32 devices in a mesh: slab: 4 (over y, x), dev: 8 (over z, core).
Axes of the slice: x: 2, y: 2, z: 4, core: 2. Of those that a mesh axis runs over, the one named last changes fastest.
Arguments:
- layer_input: bfloat16 [8, 2048, 1152], P('dev', 'slab'), may hold values from -6 to 6
- output_grad: bfloat16 [8, 2048, 1152], P('dev', 'slab'), may hold values from -6 to 6
- expert_lists: int32 [4, 8, 512], P('slab'), may hold values from 0 to 4095, as said below
- gate_values: float32 [4, 8, 512], P('slab', 'dev'), may hold values from 0.1 to 1
- weight_in: bfloat16 [8, 1152, 2304], P('dev'), may hold values from -0.1875 to 0.1875
- weight_out: bfloat16 [8, 2304, 1152], P('dev'), may hold values from -0.125 to 0.125
- query_rows: bfloat16 [8, 2048, 1152], P(None, ('slab', 'dev')), may hold values from -8 to 8
- key_rows: bfloat16 [8, 2048, 1152], P(None, ('slab', 'dev')), may hold values from -8 to 8
- value_rows: bfloat16 [8, 2048, 1152], P(None, ('slab', 'dev')), may hold values from -6 to 6
Outputs:
- gate_grad: float32 [4, 8, 512], P('slab', 'dev')
- weight_in_grad: float32 [8, 1152, 2304], P('dev', 'slab')
- weight_out_grad: float32 [8, 2304, 1152], P('dev', 'slab')
- query_grad: bfloat16 [8, 2048, 1152], P('dev', 'slab')
- key_grad: bfloat16 [8, 2048, 1152], P('dev', 'slab')
- value_grad: bfloat16 [8, 2048, 1152], P('dev', 'slab')
The draws below stay inside these ranges and needn't reach their ends.
Inputs may be any that keep to these rules, and one draw needn't show every extreme that they name: `expert_lists`: each row of a slab holds 512 distinct slab tokens. Of the 512 tokens i * 512 to (i + 1) * 512 - 1 of any frame shard i, one row takes at most 128, and every row takes exactly 128 from some frame shard.
All inputs are finite; a program needn't handle non-finite values.
Results may differ from the reference program's by a relative error of at most 0.012.
Values may be sent and summed in bfloat16 or wider, within the bound.
No kernel may reach another device: no remote copies, remote signals or barrier semaphores. Data moves between devices by JAX's collectives and lax.ppermute only.
A program may use at most 128 MiB of HBM per device.

```python
import jax
import jax.numpy as jnp
from jax import lax

D = 1152
HEADS = 16
HEAD_DIM = 72
FF = 2304
PATCH = 512
EXPERTS = 8
FRAMES = 8
SLABS = 4
PATCH_ALL = 2048
TOK_DEV = 512
SLAB_TOK = 4096
CAP = 512
SLOTS = 128


def one_expert_list(seed_key):
    key_list = jax.random.split(seed_key, 4)
    shard_count = SLAB_TOK // TOK_DEV
    half_slots = SLOTS // 2
    device_order = jax.random.permutation(key_list[0], shard_count)
    extra = jax.random.randint(key_list[1], (shard_count // 2,), 0, half_slots + 1)
    extra = extra.at[0].set(half_slots)
    counts = jnp.zeros((shard_count,), jnp.int32)
    counts = counts.at[device_order[0::2]].set(half_slots + extra)
    counts = counts.at[device_order[1::2]].set(half_slots - extra)
    shard_keys = jax.random.split(key_list[2], shard_count)
    local_orders = jax.vmap(lambda single: jax.random.permutation(single, TOK_DEV))(shard_keys)
    candidates = local_orders[:, :SLOTS] + jnp.arange(shard_count, dtype=jnp.int32)[:, None] * TOK_DEV
    usable = (jnp.arange(SLOTS, dtype=jnp.int32)[None, :] < counts[:, None]).astype(jnp.int32)
    ordering = jnp.argsort(1 - usable.reshape(-1), stable=True)[:CAP]
    chosen = candidates.reshape(-1)[ordering]
    return chosen[jax.random.permutation(key_list[3], CAP)].astype(jnp.int32)


def draw_expert_lists(key, part):
    base = jax.random.fold_in(key, 4711)
    all_keys = jax.random.split(base, SLABS * EXPERTS)
    lists_flat = jax.vmap(one_expert_list)(all_keys)
    return lists_flat.reshape(SLABS, EXPERTS, CAP).astype(jnp.int32)


def paired_fields(key):
    base = jax.random.fold_in(key, 1234)
    key_list = jax.random.split(base, 2)
    full_shape = (FRAMES, PATCH_ALL, HEADS, HEAD_DIM)
    queries = jnp.clip(jax.random.normal(key_list[0], full_shape, jnp.float32), -6.0, 6.0)
    keys_field = jnp.clip(jax.random.normal(key_list[1], full_shape, jnp.float32), -6.0, 6.0)
    return (queries.reshape(FRAMES, PATCH_ALL, D), keys_field.reshape(FRAMES, PATCH_ALL, D))


def draw_query_rows(key, part):
    return paired_fields(key)[0].astype(jnp.bfloat16)


def draw_key_rows(key, part):
    return paired_fields(key)[1].astype(jnp.bfloat16)


def block_scale(rng, dims, pieces, low, largest):
    level = 1.0
    for position, parts in pieces:
        draws = jax.random.uniform(jax.random.fold_in(jax.random.fold_in(rng, 6), position), (parts,), jnp.float32, low / len(pieces), largest / len(pieces))
        level = level * jnp.repeat(jnp.exp(draws), dims[position] // parts).reshape((-1,) + (1,) * (len(dims) - 1 - position))
    return level


def noise(rng, dims, spread, reach, shards=(), held_as=jnp.bfloat16):
    values = jax.random.normal(rng, dims, jnp.float32) * spread
    if len(shards) > 0:
        values = block_scale(rng, dims, shards, -0.22, 0.18) * values
    return jnp.clip(values, min=-reach, max=reach).astype(held_as)


def setup_inputs(seed: int = 0) -> dict:
    key_of = jax.random.split(jax.random.key(seed), 10)
    layer_input = noise(key_of[0], (FRAMES, PATCH_ALL, D), 1.0, 6.0, ((0, 8), (1, 4)))
    output_grad = noise(key_of[1], (FRAMES, PATCH_ALL, D), 1.0, 6.0, ((0, 8), (1, 4)))
    expert_lists = draw_expert_lists(jax.random.fold_in(key_of[9], 71), 0)
    gate_values = jnp.clip(0.1 + 0.9 * jax.random.uniform(key_of[3], (SLABS, EXPERTS, CAP), jnp.float32) ** block_scale(key_of[3], (SLABS, EXPERTS, CAP), ((0, 4), (1, 8)), -0.2, 0.2), 0.1, 1.0)
    weight_in = noise(key_of[4], (EXPERTS, D, FF), D ** -0.5, 0.1875, ((0, 8),))
    weight_out = noise(key_of[5], (EXPERTS, FF, D), FF ** -0.5, 0.125, ((0, 8),))
    query_rows = draw_query_rows(jax.random.fold_in(key_of[9], 71), 0)
    key_rows = draw_key_rows(jax.random.fold_in(key_of[9], 71), 0)
    value_rows = noise(key_of[8], (FRAMES, PATCH_ALL, D), 1.0, 6.0, ((1, 32),))
    return dict(layer_input=layer_input, output_grad=output_grad, expert_lists=expert_lists, gate_values=gate_values, weight_in=weight_in, weight_out=weight_out, query_rows=query_rows, key_rows=key_rows, value_rows=value_rows)


def gelu_tanh(values):
    return jax.nn.gelu(values, approximate=True)

def expert_pass(input_rows, grad_rows, gate_row, weight_first, weight_second):
    pre_act = jnp.dot(input_rows, weight_first, preferred_element_type=jnp.float32)
    act_full, pullback = jax.vjp(gelu_tanh, pre_act)
    act_rows = act_full.astype(jnp.bfloat16)
    back_proj = lax.dot_general(grad_rows, weight_second, (((1,), (1,)), ((), ())), preferred_element_type=jnp.float32)
    gate_grad = lax.optimization_barrier(jnp.sum(act_rows.astype(jnp.float32) * back_proj, axis=1))
    scaled = (gate_row[:, None] * grad_rows.astype(jnp.float32)).astype(jnp.bfloat16)
    out_term = lax.dot_general(act_rows, scaled, (((0,), (0,)), ((), ())), preferred_element_type=jnp.float32).astype(jnp.bfloat16)
    pre_grad = pullback(gate_row[:, None] * back_proj)[0].astype(jnp.bfloat16)
    in_term = lax.dot_general(input_rows, pre_grad, (((0,), (0,)), ((), ())), preferred_element_type=jnp.float32).astype(jnp.bfloat16)
    row_grad = lax.dot_general(pre_grad, weight_first, (((1,), (1,)), ((), ())), preferred_element_type=jnp.float32).astype(jnp.bfloat16)
    return (gate_grad, in_term, out_term, row_grad)

def attention_grad(query_part, key_part, value_part, grad_out):
    frame_count = query_part.shape[0]
    patch_count = query_part.shape[1]
    split_shape = (frame_count, patch_count, HEADS, HEAD_DIM)
    query_full = query_part.reshape(split_shape).astype(jnp.float32)
    key_full = key_part.reshape(split_shape).astype(jnp.float32)
    value_full = value_part.reshape(split_shape).astype(jnp.float32)
    grad_full = grad_out.reshape(split_shape).astype(jnp.float32)
    scale_factor = HEAD_DIM ** (-0.5)
    scores = jnp.einsum('fphd,gphd->phfg', query_full, key_full) * scale_factor
    attn_probs = jax.nn.softmax(scores, axis=-1)
    probs_low = lax.optimization_barrier(attn_probs.astype(jnp.bfloat16)).astype(jnp.float32)
    value_grad = jnp.einsum('phfg,fphd->gphd', probs_low, grad_full)
    prob_grad = jnp.einsum('fphd,gphd->phfg', grad_full, value_full)
    row_delta = lax.optimization_barrier(jnp.sum(attn_probs * prob_grad, axis=-1, keepdims=True))
    score_grad = lax.optimization_barrier((attn_probs * (prob_grad - row_delta)).astype(jnp.bfloat16)).astype(jnp.float32)
    query_grad = jnp.einsum('phfg,gphd->fphd', score_grad, key_full) * scale_factor
    key_grad = jnp.einsum('phfg,fphd->gphd', score_grad, query_full) * scale_factor
    flat_shape = (frame_count, patch_count, D)
    return (query_grad.reshape(flat_shape).astype(jnp.bfloat16), key_grad.reshape(flat_shape).astype(jnp.bfloat16), value_grad.reshape(flat_shape).astype(jnp.bfloat16))

def reference(layer_input, output_grad, expert_lists, gate_values, weight_in, weight_out, query_rows, key_rows, value_rows):
    gate_parts = []
    query_parts = []
    key_parts = []
    value_parts = []
    in_total = jnp.zeros((EXPERTS, D, FF), jnp.float32)
    out_total = jnp.zeros((EXPERTS, FF, D), jnp.float32)
    for slab_index in range(SLABS):
        lower = slab_index * PATCH
        upper = lower + PATCH
        slab_input = layer_input[:, lower:upper].reshape(SLAB_TOK, D)
        slab_grad = output_grad[:, lower:upper].reshape(SLAB_TOK, D)

        def per_expert(packed, slab_input=slab_input, slab_grad=slab_grad):
            chosen, gate_row, weight_first, weight_second = packed
            return expert_pass(slab_input[chosen], slab_grad[chosen], gate_row, weight_first, weight_second)
        gate_grad, in_terms, out_terms, row_grads = lax.map(per_expert, (expert_lists[slab_index], gate_values[slab_index], weight_in, weight_out))
        in_total = in_total + in_terms.astype(jnp.float32)
        out_total = out_total + out_terms.astype(jnp.float32)
        gate_parts.append(gate_grad)
        combined = jax.ops.segment_sum(row_grads.reshape(-1, D).astype(jnp.float32), expert_lists[slab_index].reshape(-1).astype(jnp.int32), num_segments=SLAB_TOK).astype(jnp.bfloat16)
        grad_attn = (slab_grad.astype(jnp.float32) + combined.astype(jnp.float32)).astype(jnp.bfloat16)
        grad_attn = grad_attn.reshape(FRAMES, PATCH, D)
        query_grad, key_grad, value_grad = attention_grad(query_rows[:, lower:upper], key_rows[:, lower:upper], value_rows[:, lower:upper], grad_attn)
        query_parts.append(query_grad)
        key_parts.append(key_grad)
        value_parts.append(value_grad)
    return (jnp.stack(gate_parts), in_total, out_total, jnp.concatenate(query_parts, axis=1), jnp.concatenate(key_parts, axis=1), jnp.concatenate(value_parts, axis=1))
```

```python
import functools

import jax
import jax.numpy as jnp
from jax import lax
from jax.experimental import pallas as pl
from jax.experimental.pallas import tpu as pltpu
from jax.sharding import PartitionSpec as P

HEADS = 16
LANES = 128
ROOT = 0.7978845608028654
CUBE = 0.044715
BF = jnp.bfloat16
F32 = jnp.float32
VMEM_LIMIT = 56 * 1024 * 1024

ROWS_COLS = (((1,), (0,)), ((), ()))
LAST_LAST = (((1,), (1,)), ((), ()))
FIRST_FIRST = (((0,), (0,)), ((), ()))


def dot(left, right, dims=ROWS_COLS):
    return lax.dot_general(left, right, dims, preferred_element_type=F32)


def call(kernel, out_shape, in_specs, args, out_specs, after=(), carry=None, flops=0, nbytes=0, **kwargs):
    held = list(after) if carry is None else [*after, carry]
    skip = len(args)
    aliases = {}
    if carry is not None:
        aliases = {skip + len(held) - 1: len(out_shape)}
        out_shape = [*out_shape, jax.ShapeDtypeStruct(carry.shape, carry.dtype)]
        out_specs = [*out_specs, ANY]

    def run(*refs):
        refs = [*refs[:skip], *refs[skip + len(held) :]]
        if carry is not None:
            del refs[skip + len(out_shape) - 1]
        kernel(*refs)

    return pl.pallas_call(
        run,
        out_shape=out_shape,
        in_specs=list(in_specs) + [ANY] * len(held),
        out_specs=out_specs,
        input_output_aliases=aliases,
        compiler_params=pltpu.CompilerParams(vmem_limit_bytes=VMEM_LIMIT),
        cost_estimate=pl.CostEstimate(flops=flops, bytes_accessed=nbytes, transcendentals=0),
        **kwargs,
    )(*args, *held)


ANY = pl.BlockSpec(memory_space=pl.ANY)
SMEM = pl.BlockSpec(memory_space=pltpu.SMEM)
WHOLE = pl.BlockSpec(memory_space=pltpu.VMEM)


def shape(dims, dtype=BF):
    return jax.ShapeDtypeStruct(dims, dtype)


def exchange_all(blocks, which, me, count):
    size = len(which)
    first = which[0]
    order = me ^ first
    groups = None
    if size < count:
        groups = [[g * size + j for j in range(size)] for g in range(count // size)]
    places = (order % size) ^ jnp.arange(size, dtype=jnp.int32)
    stacked = jnp.stack(blocks)[places]
    if first:
        across = [(i, i ^ first) for i in range(count)]
        stacked = lax.ppermute(stacked, "dev", across)
        places = (me % size) ^ jnp.arange(size, dtype=jnp.int32)
    got = lax.all_to_all(stacked, "dev", 0, 0, axis_index_groups=groups, tiled=True)[places]
    return [got[i] for i in range(size)]


def exchange_pairs(pairs, me, count):
    if count > 8:
        blocks = exchange_all([pair[j] for pair in pairs for j in range(2)], list(range(count)), me, count)
        mates = other_core(jnp.stack(blocks[1::2]), count)
        return [jnp.stack([block, mates[i]]) for i, block in enumerate(blocks[::2])]
    return [
        lax.ppermute(pair, "dev", [(d, d ^ (2 * i)) for d in range(count)]) if i else pair
        for i, pair in enumerate(pairs)
    ]


def other_core(array, count):
    return lax.ppermute(array, "dev", [(d, d ^ 1) for d in range(count)])


def exchange_single(blocks, first, me, count):
    which = list(range(first, first + len(blocks)))
    if count > 8:
        got = exchange_all([b[0] for b in blocks], which, me, count)
        return [(block[None], 0) for block in got]
    pairs = {k: [(d, d ^ k) for d in range(count)] for k in which}
    return [(lax.ppermute(b, "dev", pairs[k]) if k else b, 0) for b, k in zip(blocks, which)]


def arrays(got):
    return [array for array, _ in got]


def block_specs(got, block, index_map):
    return [
        pl.BlockSpec((None, *block), lambda *i, at=at: (at, *index_map(*i))) for _, at in got
    ]


def prep_kernel(count, group, slots, tok, me_ref, table_ref, gate_ref, x_ref, y_ref, *refs):
    send_refs = refs[:count]
    mine_ref, other_ref, gate_out, key_out, rank_ref = refs[count:]
    me = me_ref[0]
    cap = table_ref.shape[1]
    width = table_ref.shape[0]
    upper = lax.broadcasted_iota(jnp.int32, (cap, cap), 0) < lax.broadcasted_iota(
        jnp.int32, (cap, cap), 1
    )
    upper = upper.astype(F32).astype(BF)
    table = table_ref[...]
    slot_ids = lax.broadcasted_iota(jnp.int32, (slots, cap), 0)
    tok_ids = lax.broadcasted_iota(jnp.int32, (slots, tok), 1)

    def ranked(inside):
        rank = dot(inside.astype(F32).astype(BF), upper).astype(jnp.int32)
        return jnp.where(inside, rank, -1)

    def hits(frame, ks, out_ref):
        low = frame * tok
        rank_ref[...] = ranked((table >= low) & (table < low + tok))
        for place, k in enumerate(ks):
            row = rank_ref[pl.ds(me ^ k, 1), :]
            offset = table_ref[pl.ds(me ^ k, 1), :] - low
            found = jnp.where(row == slot_ids, (offset + 1).astype(F32), 0.0)
            column = (jnp.sum(found, axis=1, keepdims=True) - 1.0).astype(jnp.int32)
            out_ref[place * slots : (place + 1) * slots, :] = (
                (column == tok_ids).astype(F32).astype(BF)
            )

    hits(me, range(count), mine_ref)
    for half, source in enumerate((x_ref, y_ref)):
        rows = dot(mine_ref[...], source[...]).astype(BF)
        for k in range(count):
            send_refs[k][0, half * slots : (half + 1) * slots, :] = rows[
                k * slots : (k + 1) * slots
            ]
    hits(me ^ group, range(group), other_ref)

    mine_row = table_ref[pl.ds(me, 1), :]
    frames = (lax.broadcasted_iota(jnp.int32, (width, cap), 0) ^ me) * tok
    key = ranked((mine_row >= frames) & (mine_row < frames + tok))
    key_out[...] = key
    for k in range(count):
        found = jnp.where(key[k : k + 1, :] == slot_ids, gate_ref[...], 0.0)
        gate_out[k * slots : (k + 1) * slots, :] = jnp.sum(found, axis=1, keepdims=True)


def prep(me, table, gate_row, x, y, group):
    count, cap = table.shape
    tok, width = x.shape
    slots = 2 * cap // count
    return call(
        functools.partial(prep_kernel, count, group, slots, tok),
        [shape((1, 2 * slots, width))] * count
        + [
            shape((count * slots, tok)),
            shape((group * slots, tok)),
            shape((count * slots, 1), F32),
            shape((count, cap), jnp.int32),
        ],
        [SMEM, WHOLE, WHOLE, WHOLE, WHOLE],
        [me, table, gate_row, x, y],
        flops=4 * count * slots * tok * width,
        nbytes=8 * count * slots * width,
        out_specs=[WHOLE] * (count + 4),
        scratch_shapes=[pltpu.VMEM((count, cap), jnp.int32)],
        name="prep",
    )


def expert_kernel(parts, steps, gate_ref, first_ref, second_ref, *refs):
    in_refs = refs[:parts]
    outs = refs[parts:]
    row_refs = outs[:parts]
    x_all, scaled, act_ref, pre_ref, gg_ref, y_all, total = outs[parts:]
    step = pl.program_id(0)
    slots = in_refs[0].shape[0] // 2
    rows = parts * slots

    @pl.when(step == 0)
    def _():
        for k in range(parts):
            place = slice(k * slots, (k + 1) * slots)
            x_all[place, :] = in_refs[k][:slots, :]
            y_rows = in_refs[k][slots:, :]
            y_all[place, :] = y_rows
            scaled[place, :] = (gate_ref[place, :] * y_rows.astype(F32)).astype(BF)
        gg_ref[...] = jnp.zeros_like(gg_ref)
        total[...] = jnp.zeros_like(total)

    first = first_ref[...]
    second = second_ref[...]
    some = 128 if rows % 128 == 0 else rows
    for start in range(0, rows, some):
        place = slice(start, start + some)
        u = dot(x_all[place, :], first)
        back = dot(y_all[place, :], second, LAST_LAST)
        square = u * u
        t = jnp.tanh(u * (ROOT + (ROOT * CUBE) * square))
        half = 0.5 + 0.5 * t
        act = (u * half).astype(BF)
        slope = half + u * (1.0 - t * t) * (0.5 * ROOT + (1.5 * ROOT * CUBE) * square)
        act_ref[place, :] = act
        gg_ref[place, :] += jnp.sum(act.astype(F32) * back, axis=1, keepdims=True)
        pre = (gate_ref[place, :] * back * slope).astype(BF)
        pre_ref[place, :] = pre
        total[place, :] += dot(pre, first, LAST_LAST)

    @pl.when(step == steps - 1)
    def _():
        for k in range(parts):
            row_refs[k][0] = total[k * slots : (k + 1) * slots, :].astype(BF)


def expert(blocks, gates, weight_in, weight_out, after=()):
    parts = len(blocks)
    _, slots, width = blocks[0][0].shape
    slots //= 2
    rows = parts * slots
    hidden = weight_in.shape[1]
    tile = 768 if hidden % 768 == 0 else hidden
    steps = hidden // tile
    fixed = lambda dims: pl.BlockSpec(dims, lambda i: (0, 0))
    outs = call(
        functools.partial(expert_kernel, parts, steps),
        [shape((1, slots, width))] * parts
        + [
            shape((rows, width)),
            shape((rows, width)),
            shape((rows, hidden)),
            shape((rows, hidden)),
            shape((rows, 1), F32),
        ],
        [
            fixed((rows, 1)),
            pl.BlockSpec((width, tile), lambda i: (0, i)),
            pl.BlockSpec((tile, width), lambda i: (i, 0)),
        ]
        + block_specs(blocks, (2 * slots, width), lambda i: (0, 0)),
        [gates, weight_in, weight_out, *arrays(blocks)],
        flops=6 * rows * width * hidden,
        nbytes=4 * width * hidden + 4 * rows * hidden + 8 * rows * width,
        after=after,
        grid=(steps,),
        out_specs=[pl.BlockSpec((1, slots, width), lambda i: (0, 0, 0))] * parts
        + [
            fixed((rows, width)),
            fixed((rows, width)),
            pl.BlockSpec((rows, tile), lambda i: (0, i)),
            pl.BlockSpec((rows, tile), lambda i: (0, i)),
            fixed((rows, 1)),
        ],
        scratch_shapes=[pltpu.VMEM((rows, width), BF), pltpu.VMEM((rows, width), F32)],
        name="expert",
    )
    return outs[:parts], outs[parts:]


def weight_kernel(turn, near_left, near_right, far_left, far_right, out_ref):
    left, right = (near_left, far_left), (near_right, far_right)
    value = sum(dot(a[...], b[...], FIRST_FIRST) for a, b in zip(left, right))
    out_ref[...] = value.astype(BF)


def weight_gradient(near, far, hidden_first, after=()):
    width, hidden = near[0].shape[1], near[1].shape[1]
    tile = 768 if hidden % 768 == 0 else hidden
    args, specs = [], []
    for rows, units in (near, far):
        all_rows = pl.BlockSpec(rows.shape, lambda i: (0, 0))
        some = pl.BlockSpec((units.shape[0], tile), lambda i: (0, i))
        args += [units, rows] if hidden_first else [rows, units]
        specs += [some, all_rows] if hidden_first else [all_rows, some]
    out, out_spec = (width, hidden), pl.BlockSpec((width, tile), lambda i: (0, i))
    if hidden_first:
        out, out_spec = (hidden, width), pl.BlockSpec((tile, width), lambda i: (i, 0))
    return call(
        functools.partial(weight_kernel, hidden_first),
        shape(out),
        specs,
        args,
        flops=4 * near[0].shape[0] * width * hidden,
        nbytes=2 * width * hidden,
        after=after,
        grid=(hidden // tile,),
        out_specs=out_spec,
        name="weight_gradient",
    )


def combine_kernel(count, parts, plus, me_ref, hit_ref, *refs):
    rows = jnp.concatenate([ref[...] for ref in refs[:parts]], axis=0)
    refs = refs[parts:]
    if plus:
        y_ref, refs = refs[0], refs[1:]
    outs, total = refs[: count // 2], refs[count // 2]
    total[...] = dot(hit_ref[...], rows, FIRST_FIRST)
    piece = outs[0].shape[1]
    for k in range(count):
        place = pl.ds(pl.multiple_of((me_ref[0] ^ k) * piece, piece), piece)
        value = total[place, :]
        if plus:
            value = value + y_ref[place, :].astype(F32)
        outs[k // 2][k % 2] = value.astype(BF)


def combine(me, hit, blocks, y, count, after=(), carry=None):
    parts = len(blocks)
    _, slots, width = blocks[0][0].shape
    tok = hit.shape[1]
    plus = [] if y is None else [y]
    rows = parts * slots
    return call(
        functools.partial(combine_kernel, count, parts, bool(plus)),
        [shape((2, tok // count, width))] * (count // 2),
        [SMEM, pl.BlockSpec((rows, tok), lambda i: (0, 0))]
        + block_specs(blocks, (slots, width), lambda i: (0, 0))
        + [pl.BlockSpec(b.shape, lambda i: (0, 0)) for b in plus],
        [me, hit, *arrays(blocks), *plus],
        flops=2 * rows * tok * width,
        nbytes=6 * tok * width,
        after=after,
        carry=carry,
        grid=(1,),
        out_specs=[pl.BlockSpec((2, tok // count, width), lambda i: (0, 0, 0))] * (count // 2),
        scratch_shapes=[pltpu.VMEM((tok, width), F32)],
        name="combine",
    )


def windows(width):
    size = width // HEADS
    for head in range(HEADS):
        start, stop = head * size, (head + 1) * size
        low, high = start // LANES, -(-stop // LANES)
        yield head, start, stop, low, high, slice(low * LANES, min(high * LANES, width))


def head_lanes(start, stop, window):
    lane = lax.broadcasted_iota(jnp.int32, (1, window.stop - window.start), 1) + window.start
    return (lane >= start) & (lane < stop)


def keep(held, part, inside, low, high):
    for tile in range(low, high):
        lanes = slice((tile - low) * LANES, min((tile - low + 1) * LANES, part.shape[1]))
        new = part[:, lanes]
        if held[tile] is not None:
            new = jnp.where(inside[:, lanes], new, held[tile])
        held[tile] = new


def probs_kernel(q_ref, k_ref, probs_ref, turned_ref):
    frames, patches, width = q_ref.shape
    rows = frames * patches
    scale = (width // HEADS) ** -0.5
    query = q_ref[...].reshape(rows, width)
    keys = k_ref[...].reshape(rows, width)
    same = (lax.broadcasted_iota(jnp.int32, (rows, rows), 0) % patches) == (
        lax.broadcasted_iota(jnp.int32, (rows, rows), 1) % patches
    )
    for head, start, stop, low, high, window in windows(width):
        inside = head_lanes(start, stop, window)
        q_win = jnp.where(inside, query[:, window], jnp.zeros((), BF))
        scores = jnp.where(same, dot(q_win, keys[:, window], LAST_LAST) * scale, -1e30)
        probs = jnp.exp(scores - jnp.max(scores, axis=1, keepdims=True))
        probs = probs / jnp.sum(probs, axis=1, keepdims=True)
        probs_ref[0, head] = probs
        turned_ref[0, head] = probs.T.astype(BF)


def patch_tile(frames, patches):
    return 16 if patches % 16 == 0 else patches


def probabilities(query, keys, after=()):
    frames, patches, width = query.shape
    tile = patch_tile(frames, patches)
    steps = patches // tile
    rows = frames * tile
    wide = pl.BlockSpec((frames, tile, width), lambda i: (0, i, 0))
    square = pl.BlockSpec((1, HEADS, rows, rows), lambda i: (i, 0, 0, 0))
    return call(
        probs_kernel,
        [shape((steps, HEADS, rows, rows), F32), shape((steps, HEADS, rows, rows))],
        [wide, wide],
        [query, keys],
        flops=8 * frames * patches * rows * width,
        nbytes=4 * frames * patches * width + 6 * steps * HEADS * rows * rows,
        after=after,
        grid=(steps,),
        out_specs=[square, square],
        name="probs",
    )


def meet_kernel(chips, *refs):
    near, far, out_ref = refs[:chips], refs[chips : 2 * chips], refs[2 * chips]
    for i in range(chips):
        value = near[i][...].astype(F32) + far[i ^ (chips // 2)][...].astype(F32)
        out_ref[i] = value.astype(BF)


def meet(near, far, carry):
    chips = len(near)
    _, piece, width = near[0].shape
    spec = pl.BlockSpec((None, piece, width), lambda i: (1, 0, 0))
    return call(
        functools.partial(meet_kernel, chips),
        [shape((chips, piece, width))],
        [spec] * (2 * chips),
        [*near, *far],
        nbytes=6 * chips * piece * width,
        carry=carry,
        grid=(1,),
        out_specs=[pl.BlockSpec((chips, piece, width), lambda i: (0, 0, 0))],
        name="meet",
    )


def value_kernel(count, me_ref, turned_ref, odd_ref, *refs):
    chips = count // 2
    near, far, refs = refs[:chips], refs[chips : 2 * chips], refs[2 * chips :]
    outs = refs[:count]
    grad_ref, result = refs[count:]
    me = me_ref[0]
    frames, patches, width = grad_ref.shape
    rows = frames * patches
    for i in range(chips):
        value = near[i][...].astype(F32) + far[i ^ (chips // 2)][...].astype(F32)
        grad_ref[me ^ (2 * i)] = value.astype(BF)
        grad_ref[me ^ (2 * i + 1)] = odd_ref[i]
    grad = grad_ref[...].reshape(rows, width)
    held = [None] * -(-width // LANES)
    for head, start, stop, low, high, window in windows(width):
        inside = head_lanes(start, stop, window)
        keep(held, dot(turned_ref[0, head], grad[:, window]), inside, low, high)
    for tile, value in enumerate(held):
        lanes = slice(tile * LANES, tile * LANES + value.shape[1])
        result[:, :, lanes] = value.astype(BF).reshape(frames, patches, value.shape[1])
    for k in range(count):
        outs[k][0] = result[me ^ k]


def value_gradient(me, turned, odd, near, far, count, after=()):
    _, piece, width = near[0].shape
    steps, _, rows, _ = turned.shape
    tile = piece // steps
    frames = rows // tile
    wide = pl.BlockSpec((frames, tile, width), lambda i: (0, i, 0))
    even = pl.BlockSpec((None, tile, width), lambda i: (0, i, 0))
    outs = call(
        functools.partial(value_kernel, count),
        [shape((1, piece, width))] * count + [shape((frames, piece, width))],
        [
            SMEM,
            pl.BlockSpec((1, HEADS, rows, rows), lambda i: (i, 0, 0, 0)),
            pl.BlockSpec((count // 2, tile, width), lambda i: (0, i, 0)),
        ]
        + [even] * (2 * len(near)),
        [me, turned, odd, *near, *far],
        flops=4 * frames * piece * rows * width,
        nbytes=8 * frames * piece * width,
        after=after,
        grid=(steps,),
        out_specs=[pl.BlockSpec((1, tile, width), lambda i: (0, i, 0))] * count + [wide],
        scratch_shapes=[pltpu.VMEM((frames, tile, width), BF)],
        name="value_gradient",
    )
    return outs[:count], outs[count]


def pair_kernel(count, me_ref, probs_ref, grad_ref, q_ref, k_ref, v_ref, *refs):
    outs, result = refs[:count], refs[count]
    me = me_ref[0]
    frames, patches, width = q_ref.shape
    rows = frames * patches
    scale = (width // HEADS) ** -0.5
    query, keys, values, grad = (
        ref[...].reshape(rows, width) for ref in (q_ref, k_ref, v_ref, grad_ref)
    )
    tiles = -(-width // LANES)
    held = [[None] * tiles for _ in range(2)]
    for head, start, stop, low, high, window in windows(width):
        inside = head_lanes(start, stop, window)
        g_win = jnp.where(inside, grad[:, window], jnp.zeros((), BF))
        prob_grad = dot(g_win, values[:, window], LAST_LAST)
        probs = probs_ref[0, head]
        delta = jnp.sum(probs * prob_grad, axis=1, keepdims=True)
        score_grad = (probs * (prob_grad - delta)).astype(BF)
        keep(held[0], dot(score_grad, keys[:, window]) * scale, inside, low, high)
        keep(held[1], dot(score_grad, query[:, window], FIRST_FIRST) * scale, inside, low, high)
    for which in range(2):
        for tile, value in enumerate(held[which]):
            lanes = slice(tile * LANES, tile * LANES + value.shape[1])
            value = value.astype(BF).reshape(frames, patches, value.shape[1])
            result[which, :, :, lanes] = value
    for k in range(count):
        for which in range(2):
            outs[k][0, which] = result[which, me ^ k]


def pair_gradients(me, probs, grad, query, keys, values, count, after=()):
    frames, piece, width = query.shape
    steps, _, rows, _ = probs.shape
    tile = piece // steps
    wide = pl.BlockSpec((frames, tile, width), lambda i: (0, i, 0))
    return call(
        functools.partial(pair_kernel, count),
        [shape((1, 2, piece, width))] * count,
        [SMEM, pl.BlockSpec((1, HEADS, rows, rows), lambda i: (i, 0, 0, 0))] + [wide] * 4,
        [me, probs, grad, query, keys, values],
        flops=12 * frames * piece * rows * width,
        nbytes=16 * frames * piece * width,
        after=after,
        grid=(steps,),
        out_specs=[pl.BlockSpec((1, 2, tile, width), lambda i: (0, 0, i, 0))] * count,
        scratch_shapes=[pltpu.VMEM((2, frames, tile, width), BF)],
        name="pair_gradients",
    )


def place_kernel(count, outs_count, me_ref, *refs):
    blocks, outs = refs[:count][::-1], refs[count:]
    piece = blocks[0].shape[-2]
    for k in range(count):
        place = pl.ds(pl.multiple_of((me_ref[0] ^ k) * piece, piece), piece)
        if outs_count == 1:
            outs[0][place, :] = blocks[k][...]
        else:
            for which in range(outs_count):
                outs[which][place, :] = blocks[k][which]


def place(me, blocks, after=()):
    count = len(blocks)
    dims = blocks[0][0].shape[1:]
    tok = count * dims[-2]
    outs_count = dims[0] if len(dims) == 3 else 1
    return call(
        functools.partial(place_kernel, count, outs_count),
        [shape((tok, dims[-1]))] * outs_count,
        [SMEM] + block_specs(blocks[::-1], dims, lambda i: (0,) * len(dims)),
        [me, *arrays(blocks[::-1])],
        nbytes=4 * outs_count * tok * dims[-1],
        after=after,
        grid=(1,),
        out_specs=[pl.BlockSpec((tok, dims[-1]), lambda i: (0, 0))] * outs_count,
        name="place",
    )


def body(
    layer_input,
    output_grad,
    expert_lists,
    gate_values,
    weight_in,
    weight_out,
    query_rows,
    key_rows,
    value_rows,
):
    count = lax.axis_size("dev")
    index = lax.axis_index("dev").astype(jnp.int32)
    me = index.reshape(1)
    frames_here, patches, width = layer_input.shape
    tok = frames_here * patches
    cap = expert_lists.shape[2]
    group = count // 2
    x = layer_input.reshape(tok, width)
    y = output_grad.reshape(tok, width)
    first, second = weight_in[0], weight_out[0]
    pairs = functools.partial(exchange_pairs, me=index, count=count)

    *send, hit_mine, hit_other, gates, key = prep(
        me, expert_lists[0], gate_values[0], x, y, group
    )
    slots = send[0].shape[1] // 2
    half = group * slots
    single = functools.partial(exchange_single, me=index, count=count)
    got_near = single(send[:group], 0)
    got_far = single(send[group:], group)

    probs, turned = probabilities(query_rows, key_rows, after=[hit_mine])
    rows_near, rest_near = expert(
        got_near, gates[:half], first, second, after=[turned, *arrays(got_far[: group // 2])]
    )
    back_near = single(rows_near, 0)
    send_near = combine(me, hit_mine, back_near, y, count, after=arrays(got_far[group // 2 :]))
    grad_near = pairs(send_near)
    rows_far, rest_far = expert(got_far, gates[half:], first, second, after=send_near[:1])
    back_far = single(rows_far, 0)

    x_near, scaled_near, act_near, pre_near, sums_near = rest_near
    x_far, scaled_far, act_far, pre_far, sums_far = rest_far
    crossed = grad_near[1:]
    in_term = weight_gradient((x_near, pre_near), (x_far, pre_far), False, after=crossed)
    *send_far, in_term = combine(me, hit_other, back_far, None, count, carry=in_term)
    in_share = lax.psum_scatter(in_term, "slab", scatter_dimension=0, tiled=True).astype(F32)
    grad_far = pairs(send_far)
    out_term = weight_gradient(
        (scaled_near, act_near), (scaled_far, act_far), True, after=send_far[:1]
    )
    slot_sums = jnp.concatenate([sums_near, sums_far]).reshape(count, slots, 1)
    slot_ids = jnp.arange(slots, dtype=jnp.int32)[None, :, None]
    gate_grad = jnp.sum(jnp.where(key[:, None, :] == slot_ids, slot_sums, 0.0), axis=(0, 1))

    odd, out_term = meet(grad_near, grad_far, out_term)
    out_share = lax.psum_scatter(out_term, "slab", scatter_dimension=0, tiled=True).astype(F32)
    odd = other_core(odd, count)
    value_send, grad_attn = value_gradient(me, turned, odd, grad_near, grad_far, count)
    pair_send = pair_gradients(me, probs, grad_attn, query_rows, key_rows, value_rows, count)
    (value_grad,) = place(me, single(value_send, 0), after=pair_send[:1])
    query_grad, key_grad = place(me, single(pair_send, 0))
    whole = (frames_here, patches, width)
    return (
        gate_grad.reshape(1, 1, cap),
        in_share[None],
        out_share[None],
        query_grad.reshape(whole),
        key_grad.reshape(whole),
        value_grad.reshape(whole),
    )


def solution(mesh):
    return jax.shard_map(
        body,
        mesh=mesh,
        in_specs=(
            P("dev", "slab", None),
            P("dev", "slab", None),
            P("slab", None, None),
            P("slab", "dev", None),
            P("dev", None, None),
            P("dev", None, None),
            P(None, ("slab", "dev"), None),
            P(None, ("slab", "dev"), None),
            P(None, ("slab", "dev"), None),
        ),
        out_specs=(
            P("slab", "dev", None),
            P("dev", "slab", None),
            P("dev", "slab", None),
            P("dev", "slab", None),
            P("dev", "slab", None),
            P("dev", "slab", None),
        ),
        check_vma=False,
    )
```

```python
import functools

import jax
import jax.numpy as jnp
from jax import lax
from jax.experimental import pallas as pl
from jax.experimental.pallas import tpu as pltpu
from jax.sharding import PartitionSpec as P

HEADS = 16
LANES = 128
ROOT = 0.7978845608028654
CUBE = 0.044715
BF = jnp.bfloat16
F32 = jnp.float32
VMEM_LIMIT = 56 * 1024 * 1024

ROWS_COLS = (((1,), (0,)), ((), ()))
LAST_LAST = (((1,), (1,)), ((), ()))
FIRST_FIRST = (((0,), (0,)), ((), ()))


def dot(left, right, dims=ROWS_COLS):
    return lax.dot_general(left, right, dims, preferred_element_type=F32)


def call(kernel, out_shape, in_specs, args, out_specs, after=(), carry=None, flops=0, nbytes=0, **kwargs):
    held = list(after) if carry is None else [*after, carry]
    skip = len(args)
    aliases = {}
    if carry is not None:
        aliases = {skip + len(held) - 1: len(out_shape)}
        out_shape = [*out_shape, jax.ShapeDtypeStruct(carry.shape, carry.dtype)]
        out_specs = [*out_specs, ANY]

    def run(*refs):
        refs = [*refs[:skip], *refs[skip + len(held) :]]
        if carry is not None:
            del refs[skip + len(out_shape) - 1]
        kernel(*refs)

    return pl.pallas_call(
        run,
        out_shape=out_shape,
        in_specs=list(in_specs) + [ANY] * len(held),
        out_specs=out_specs,
        input_output_aliases=aliases,
        compiler_params=pltpu.CompilerParams(vmem_limit_bytes=VMEM_LIMIT),
        cost_estimate=pl.CostEstimate(flops=flops, bytes_accessed=nbytes, transcendentals=0),
        **kwargs,
    )(*args, *held)


ANY = pl.BlockSpec(memory_space=pl.ANY)
SMEM = pl.BlockSpec(memory_space=pltpu.SMEM)
WHOLE = pl.BlockSpec(memory_space=pltpu.VMEM)


def shape(dims, dtype=BF):
    return jax.ShapeDtypeStruct(dims, dtype)


def exchange_all(blocks, which, me, count):
    size = len(which)
    first = which[0]
    order = me ^ first
    groups = None
    if size < count:
        groups = [[g * size + j for j in range(size)] for g in range(count // size)]
    places = (order % size) ^ jnp.arange(size, dtype=jnp.int32)
    stacked = jnp.stack(blocks)[places]
    if first:
        across = [(i, i ^ first) for i in range(count)]
        stacked = lax.ppermute(stacked, "dev", across)
        places = (me % size) ^ jnp.arange(size, dtype=jnp.int32)
    got = lax.all_to_all(stacked, "dev", 0, 0, axis_index_groups=groups, tiled=True)[places]
    return [got[i] for i in range(size)]


def exchange_pairs(pairs, me, count):
    if count > 8:
        blocks = exchange_all([pair[j] for pair in pairs for j in range(2)], list(range(count)), me, count)
        mates = other_core(jnp.stack(blocks[1::2]), count)
        return [jnp.stack([block, mates[i]]) for i, block in enumerate(blocks[::2])]
    return [
        lax.ppermute(pair, "dev", [(d, d ^ (2 * i)) for d in range(count)]) if i else pair
        for i, pair in enumerate(pairs)
    ]


def other_core(array, count):
    return lax.ppermute(array, "dev", [(d, d ^ 1) for d in range(count)])


def exchange_single(blocks, first, me, count):
    which = list(range(first, first + len(blocks)))
    if count > 8:
        got = exchange_all([b[0] for b in blocks], which, me, count)
        return [(block[None], 0) for block in got]
    pairs = {k: [(d, d ^ k) for d in range(count)] for k in which}
    return [(lax.ppermute(b, "dev", pairs[k]) if k else b, 0) for b, k in zip(blocks, which)]


def exchange_apart(block, k, count):
    pairs = [(d, d ^ k) for d in range(count)]
    far = [(d, e) for d, e in pairs if abs(d - e) > count // 2]
    near = [(d, e) for d, e in pairs if abs(d - e) <= count // 2]
    return lax.ppermute(block, "dev", far), lax.ppermute(block, "dev", near)


def arrays(got):
    return [array for array, _ in got]


def block_specs(got, block, index_map):
    return [
        pl.BlockSpec((None, *block), lambda *i, at=at: (at, *index_map(*i))) for _, at in got
    ]


def prep_kernel(count, group, slots, tok, me_ref, table_ref, gate_ref, x_ref, y_ref, *refs):
    send_refs = refs[:count]
    mine_ref, other_ref, gate_out, key_out, rank_ref = refs[count:]
    me = me_ref[0]
    cap = table_ref.shape[1]
    width = table_ref.shape[0]
    upper = lax.broadcasted_iota(jnp.int32, (cap, cap), 0) < lax.broadcasted_iota(
        jnp.int32, (cap, cap), 1
    )
    upper = upper.astype(F32).astype(BF)
    table = table_ref[...]
    slot_ids = lax.broadcasted_iota(jnp.int32, (slots, cap), 0)
    tok_ids = lax.broadcasted_iota(jnp.int32, (slots, tok), 1)

    def ranked(inside):
        rank = dot(inside.astype(F32).astype(BF), upper).astype(jnp.int32)
        return jnp.where(inside, rank, -1)

    def hits(frame, ks, out_ref):
        low = frame * tok
        rank_ref[...] = ranked((table >= low) & (table < low + tok))
        for place, k in enumerate(ks):
            row = rank_ref[pl.ds(me ^ k, 1), :]
            offset = table_ref[pl.ds(me ^ k, 1), :] - low
            found = jnp.where(row == slot_ids, (offset + 1).astype(F32), 0.0)
            column = (jnp.sum(found, axis=1, keepdims=True) - 1.0).astype(jnp.int32)
            out_ref[place * slots : (place + 1) * slots, :] = (
                (column == tok_ids).astype(F32).astype(BF)
            )

    hits(me, range(count), mine_ref)
    for half, source in enumerate((x_ref, y_ref)):
        rows = dot(mine_ref[...], source[...]).astype(BF)
        for k in range(count):
            send_refs[k][0, half * slots : (half + 1) * slots, :] = rows[
                k * slots : (k + 1) * slots
            ]
    hits(me ^ group, range(group), other_ref)

    mine_row = table_ref[pl.ds(me, 1), :]
    frames = (lax.broadcasted_iota(jnp.int32, (width, cap), 0) ^ me) * tok
    key = ranked((mine_row >= frames) & (mine_row < frames + tok))
    key_out[...] = key
    for k in range(count):
        found = jnp.where(key[k : k + 1, :] == slot_ids, gate_ref[...], 0.0)
        gate_out[k * slots : (k + 1) * slots, :] = jnp.sum(found, axis=1, keepdims=True)


def prep(me, table, gate_row, x, y, group):
    count, cap = table.shape
    tok, width = x.shape
    slots = 2 * cap // count
    return call(
        functools.partial(prep_kernel, count, group, slots, tok),
        [shape((1, 2 * slots, width))] * count
        + [
            shape((count * slots, tok)),
            shape((group * slots, tok)),
            shape((count * slots, 1), F32),
            shape((count, cap), jnp.int32),
        ],
        [SMEM, WHOLE, WHOLE, WHOLE, WHOLE],
        [me, table, gate_row, x, y],
        flops=4 * count * slots * tok * width,
        nbytes=8 * count * slots * width,
        out_specs=[WHOLE] * (count + 4),
        scratch_shapes=[pltpu.VMEM((count, cap), jnp.int32)],
        name="prep",
    )


def expert_kernel(parts, steps, apart, gate_ref, first_ref, second_ref, *refs):
    in_refs = refs[:parts]
    more_refs = dict(zip(apart, refs[parts:]))
    outs = refs[parts + len(apart) :]
    row_refs = outs[:parts]
    x_all, scaled, act_ref, pre_ref, gg_ref, y_all, total = outs[parts:]
    step = pl.program_id(0)
    slots = in_refs[0].shape[0] // 2

    @pl.when(step == 0)
    def _():
        for k in range(parts):
            place = slice(k * slots, (k + 1) * slots)
            value = in_refs[k][...]
            if k in more_refs:
                value = value + more_refs[k][...]
            x_all[place, :] = value[:slots, :]
            y_rows = value[slots:, :]
            y_all[place, :] = y_rows
            scaled[place, :] = (gate_ref[place, :] * y_rows.astype(F32)).astype(BF)
        gg_ref[...] = jnp.zeros_like(gg_ref)
        total[...] = jnp.zeros_like(total)

    first = first_ref[...]
    second = second_ref[...]
    u = dot(x_all[...], first)
    back = dot(y_all[...], second, LAST_LAST)
    square = u * u
    t = jnp.tanh(u * (ROOT + (ROOT * CUBE) * square))
    half = 0.5 + 0.5 * t
    act = (u * half).astype(BF)
    slope = half + u * (1.0 - t * t) * (0.5 * ROOT + (1.5 * ROOT * CUBE) * square)
    act_ref[...] = act
    gg_ref[...] += jnp.sum(act.astype(F32) * back, axis=1, keepdims=True)
    pre = (gate_ref[...] * back * slope).astype(BF)
    pre_ref[...] = pre
    total[...] += dot(pre, first, LAST_LAST)

    @pl.when(step == steps - 1)
    def _():
        for k in range(parts):
            row_refs[k][0] = total[k * slots : (k + 1) * slots, :].astype(BF)


def expert(blocks, gates, weight_in, weight_out, more=(), after=()):
    more = dict(more)
    parts = len(blocks)
    _, slots, width = blocks[0][0].shape
    slots //= 2
    rows = parts * slots
    hidden = weight_in.shape[1]
    tile = 768 if hidden % 768 == 0 else hidden
    steps = hidden // tile
    fixed = lambda dims: pl.BlockSpec(dims, lambda i: (0, 0))
    outs = call(
        functools.partial(expert_kernel, parts, steps, tuple(more)),
        [shape((1, slots, width))] * parts
        + [
            shape((rows, width)),
            shape((rows, width)),
            shape((rows, hidden)),
            shape((rows, hidden)),
            shape((rows, 1), F32),
        ],
        [
            fixed((rows, 1)),
            pl.BlockSpec((width, tile), lambda i: (0, i)),
            pl.BlockSpec((tile, width), lambda i: (i, 0)),
        ]
        + block_specs([*blocks, *more.values()], (2 * slots, width), lambda i: (0, 0)),
        [gates, weight_in, weight_out, *arrays(blocks), *arrays(more.values())],
        flops=6 * rows * width * hidden,
        nbytes=4 * width * hidden + 4 * rows * hidden + 8 * rows * width,
        after=after,
        grid=(steps,),
        out_specs=[pl.BlockSpec((1, slots, width), lambda i: (0, 0, 0))] * parts
        + [
            fixed((rows, width)),
            fixed((rows, width)),
            pl.BlockSpec((rows, tile), lambda i: (0, i)),
            pl.BlockSpec((rows, tile), lambda i: (0, i)),
            fixed((rows, 1)),
        ],
        scratch_shapes=[pltpu.VMEM((rows, width), BF), pltpu.VMEM((rows, width), F32)],
        name="expert",
    )
    return outs[:parts], outs[parts:]


def weight_kernel(turn, near_left, near_right, far_left, far_right, out_ref):
    left, right = (near_left, far_left), (near_right, far_right)
    value = sum(dot(a[...], b[...], FIRST_FIRST) for a, b in zip(left, right))
    out_ref[...] = value.astype(BF)


def weight_gradient(near, far, hidden_first, after=()):
    width, hidden = near[0].shape[1], near[1].shape[1]
    tile = 768 if hidden % 768 == 0 else hidden
    args, specs = [], []
    for rows, units in (near, far):
        all_rows = pl.BlockSpec(rows.shape, lambda i: (0, 0))
        some = pl.BlockSpec((units.shape[0], tile), lambda i: (0, i))
        args += [units, rows] if hidden_first else [rows, units]
        specs += [some, all_rows] if hidden_first else [all_rows, some]
    out, out_spec = (width, hidden), pl.BlockSpec((width, tile), lambda i: (0, i))
    if hidden_first:
        out, out_spec = (hidden, width), pl.BlockSpec((tile, width), lambda i: (i, 0))
    return call(
        functools.partial(weight_kernel, hidden_first),
        shape(out),
        specs,
        args,
        flops=4 * near[0].shape[0] * width * hidden,
        nbytes=2 * width * hidden,
        after=after,
        grid=(hidden // tile,),
        out_specs=out_spec,
        name="weight_gradient",
    )


def combine_kernel(count, parts, plus, me_ref, hit_ref, *refs):
    rows = jnp.concatenate([ref[...] for ref in refs[:parts]], axis=0)
    refs = refs[parts:]
    if plus:
        y_ref, refs = refs[0], refs[1:]
    outs, total = refs[: count // 2], refs[count // 2]
    total[...] = dot(hit_ref[...], rows, FIRST_FIRST)
    piece = outs[0].shape[1]
    for k in range(count):
        place = pl.ds(pl.multiple_of((me_ref[0] ^ k) * piece, piece), piece)
        value = total[place, :]
        if plus:
            value = value + y_ref[place, :].astype(F32)
        outs[k // 2][k % 2] = value.astype(BF)


def combine(me, hit, blocks, y, count, after=(), carry=None):
    parts = len(blocks)
    _, slots, width = blocks[0][0].shape
    tok = hit.shape[1]
    plus = [] if y is None else [y]
    rows = parts * slots
    return call(
        functools.partial(combine_kernel, count, parts, bool(plus)),
        [shape((2, tok // count, width))] * (count // 2),
        [SMEM, pl.BlockSpec((rows, tok), lambda i: (0, 0))]
        + block_specs(blocks, (slots, width), lambda i: (0, 0))
        + [pl.BlockSpec(b.shape, lambda i: (0, 0)) for b in plus],
        [me, hit, *arrays(blocks), *plus],
        flops=2 * rows * tok * width,
        nbytes=6 * tok * width,
        after=after,
        carry=carry,
        grid=(1,),
        out_specs=[pl.BlockSpec((2, tok // count, width), lambda i: (0, 0, 0))] * (count // 2),
        scratch_shapes=[pltpu.VMEM((tok, width), F32)],
        name="combine",
    )


def windows(width):
    size = width // HEADS
    for head in range(HEADS):
        start, stop = head * size, (head + 1) * size
        low, high = start // LANES, -(-stop // LANES)
        yield head, start, stop, low, high, slice(low * LANES, min(high * LANES, width))


def head_lanes(start, stop, window):
    lane = lax.broadcasted_iota(jnp.int32, (1, window.stop - window.start), 1) + window.start
    return (lane >= start) & (lane < stop)


def keep(held, part, inside, low, high):
    for tile in range(low, high):
        lanes = slice((tile - low) * LANES, min((tile - low + 1) * LANES, part.shape[1]))
        new = part[:, lanes]
        if held[tile] is not None:
            new = jnp.where(inside[:, lanes], new, held[tile])
        held[tile] = new


def probs_kernel(q_ref, k_ref, probs_ref, turned_ref):
    frames, patches, width = q_ref.shape
    rows = frames * patches
    scale = (width // HEADS) ** -0.5
    query = q_ref[...].reshape(rows, width)
    keys = k_ref[...].reshape(rows, width)
    same = (lax.broadcasted_iota(jnp.int32, (rows, rows), 0) % patches) == (
        lax.broadcasted_iota(jnp.int32, (rows, rows), 1) % patches
    )
    for head, start, stop, low, high, window in windows(width):
        inside = head_lanes(start, stop, window)
        q_win = jnp.where(inside, query[:, window], jnp.zeros((), BF))
        scores = jnp.where(same, dot(q_win, keys[:, window], LAST_LAST) * scale, -1e30)
        probs = jnp.exp(scores - jnp.max(scores, axis=1, keepdims=True))
        probs = probs / jnp.sum(probs, axis=1, keepdims=True)
        probs_ref[0, head] = probs
        turned_ref[0, head] = probs.T.astype(BF)


def patch_tile(frames, patches):
    return 16 if patches % 16 == 0 else patches


def probabilities(query, keys, after=()):
    frames, patches, width = query.shape
    tile = patch_tile(frames, patches)
    steps = patches // tile
    rows = frames * tile
    wide = pl.BlockSpec((frames, tile, width), lambda i: (0, i, 0))
    square = pl.BlockSpec((1, HEADS, rows, rows), lambda i: (i, 0, 0, 0))
    return call(
        probs_kernel,
        [shape((steps, HEADS, rows, rows), F32), shape((steps, HEADS, rows, rows))],
        [wide, wide],
        [query, keys],
        flops=8 * frames * patches * rows * width,
        nbytes=4 * frames * patches * width + 6 * steps * HEADS * rows * rows,
        after=after,
        grid=(steps,),
        out_specs=[square, square],
        name="probs",
    )


def meet_kernel(chips, *refs):
    near, far, out_ref = refs[:chips], refs[chips : 2 * chips], refs[2 * chips]
    for i in range(chips):
        value = near[i][...].astype(F32) + far[i ^ (chips // 2)][...].astype(F32)
        out_ref[i] = value.astype(BF)


def meet(near, far, carry):
    chips = len(near)
    _, piece, width = near[0].shape
    spec = pl.BlockSpec((None, piece, width), lambda i: (1, 0, 0))
    return call(
        functools.partial(meet_kernel, chips),
        [shape((chips, piece, width))],
        [spec] * (2 * chips),
        [*near, *far],
        nbytes=6 * chips * piece * width,
        carry=carry,
        grid=(1,),
        out_specs=[pl.BlockSpec((chips, piece, width), lambda i: (0, 0, 0))],
        name="meet",
    )


def value_kernel(count, me_ref, turned_ref, odd_ref, *refs):
    chips = count // 2
    near, far, refs = refs[:chips], refs[chips : 2 * chips], refs[2 * chips :]
    outs = refs[:count]
    grad_ref, result = refs[count:]
    me = me_ref[0]
    frames, patches, width = grad_ref.shape
    rows = frames * patches
    for i in range(chips):
        value = near[i][...].astype(F32) + far[i ^ (chips // 2)][...].astype(F32)
        grad_ref[me ^ (2 * i)] = value.astype(BF)
        grad_ref[me ^ (2 * i + 1)] = odd_ref[i]
    grad = grad_ref[...].reshape(rows, width)
    held = [None] * -(-width // LANES)
    for head, start, stop, low, high, window in windows(width):
        inside = head_lanes(start, stop, window)
        keep(held, dot(turned_ref[0, head], grad[:, window]), inside, low, high)
    for tile, value in enumerate(held):
        lanes = slice(tile * LANES, tile * LANES + value.shape[1])
        result[:, :, lanes] = value.astype(BF).reshape(frames, patches, value.shape[1])
    for k in range(count):
        outs[k][0] = result[me ^ k]


def value_gradient(me, turned, odd, near, far, count, after=()):
    _, piece, width = near[0].shape
    steps, _, rows, _ = turned.shape
    tile = piece // steps
    frames = rows // tile
    wide = pl.BlockSpec((frames, tile, width), lambda i: (0, i, 0))
    even = pl.BlockSpec((None, tile, width), lambda i: (0, i, 0))
    outs = call(
        functools.partial(value_kernel, count),
        [shape((1, piece, width))] * count + [shape((frames, piece, width))],
        [
            SMEM,
            pl.BlockSpec((1, HEADS, rows, rows), lambda i: (i, 0, 0, 0)),
            pl.BlockSpec((count // 2, tile, width), lambda i: (0, i, 0)),
        ]
        + [even] * (2 * len(near)),
        [me, turned, odd, *near, *far],
        flops=4 * frames * piece * rows * width,
        nbytes=8 * frames * piece * width,
        after=after,
        grid=(steps,),
        out_specs=[pl.BlockSpec((1, tile, width), lambda i: (0, i, 0))] * count + [wide],
        scratch_shapes=[pltpu.VMEM((frames, tile, width), BF)],
        name="value_gradient",
    )
    return outs[:count], outs[count]


def pair_kernel(count, me_ref, probs_ref, grad_ref, q_ref, k_ref, v_ref, *refs):
    outs, result = refs[:count], refs[count]
    me = me_ref[0]
    frames, patches, width = q_ref.shape
    rows = frames * patches
    scale = (width // HEADS) ** -0.5
    query, keys, values, grad = (
        ref[...].reshape(rows, width) for ref in (q_ref, k_ref, v_ref, grad_ref)
    )
    tiles = -(-width // LANES)
    held = [[None] * tiles for _ in range(2)]
    for head, start, stop, low, high, window in windows(width):
        inside = head_lanes(start, stop, window)
        g_win = jnp.where(inside, grad[:, window], jnp.zeros((), BF))
        prob_grad = dot(g_win, values[:, window], LAST_LAST)
        probs = probs_ref[0, head]
        delta = jnp.sum(probs * prob_grad, axis=1, keepdims=True)
        score_grad = (probs * (prob_grad - delta)).astype(BF)
        keep(held[0], dot(score_grad, keys[:, window]) * scale, inside, low, high)
        keep(held[1], dot(score_grad, query[:, window], FIRST_FIRST) * scale, inside, low, high)
    for which in range(2):
        for tile, value in enumerate(held[which]):
            lanes = slice(tile * LANES, tile * LANES + value.shape[1])
            value = value.astype(BF).reshape(frames, patches, value.shape[1])
            result[which, :, :, lanes] = value
    for k in range(count):
        for which in range(2):
            outs[k][0, which] = result[which, me ^ k]


def pair_gradients(me, probs, grad, query, keys, values, count, after=()):
    frames, piece, width = query.shape
    steps, _, rows, _ = probs.shape
    tile = piece // steps
    wide = pl.BlockSpec((frames, tile, width), lambda i: (0, i, 0))
    return call(
        functools.partial(pair_kernel, count),
        [shape((1, 2, piece, width))] * count,
        [SMEM, pl.BlockSpec((1, HEADS, rows, rows), lambda i: (i, 0, 0, 0))] + [wide] * 4,
        [me, probs, grad, query, keys, values],
        flops=12 * frames * piece * rows * width,
        nbytes=16 * frames * piece * width,
        after=after,
        grid=(steps,),
        out_specs=[pl.BlockSpec((1, 2, tile, width), lambda i: (0, 0, i, 0))] * count,
        scratch_shapes=[pltpu.VMEM((2, frames, tile, width), BF)],
        name="pair_gradients",
    )


def spread(count):
    half, quarter = count // 2, count // 4
    far = [k for i in range(quarter) for k in (half + quarter + i, half + i)]
    return far + list(range(half - 1, -1, -1))


def place_kernel(order, outs_count, me_ref, *refs):
    blocks, outs = refs[: len(order)], refs[len(order) :]
    piece = blocks[0].shape[-2]
    for k, block in zip(order, blocks):
        place = pl.ds(pl.multiple_of((me_ref[0] ^ k) * piece, piece), piece)
        if outs_count == 1:
            outs[0][place, :] = block[...]
        else:
            for which in range(outs_count):
                outs[which][place, :] = block[which]


def place(me, blocks, after=()):
    count = len(blocks)
    dims = blocks[0][0].shape[1:]
    tok = count * dims[-2]
    outs_count = dims[0] if len(dims) == 3 else 1
    order = spread(count)
    blocks = [blocks[k] for k in order]
    return call(
        functools.partial(place_kernel, order, outs_count),
        [shape((tok, dims[-1]))] * outs_count,
        [SMEM] + block_specs(blocks, dims, lambda i: (0,) * len(dims)),
        [me, *arrays(blocks)],
        nbytes=4 * outs_count * tok * dims[-1],
        after=after,
        grid=(1,),
        out_specs=[pl.BlockSpec((tok, dims[-1]), lambda i: (0, 0))] * outs_count,
        name="place",
    )


def body(
    layer_input,
    output_grad,
    expert_lists,
    gate_values,
    weight_in,
    weight_out,
    query_rows,
    key_rows,
    value_rows,
):
    count = lax.axis_size("dev")
    index = lax.axis_index("dev").astype(jnp.int32)
    me = index.reshape(1)
    frames_here, patches, width = layer_input.shape
    tok = frames_here * patches
    cap = expert_lists.shape[2]
    group = count // 2
    x = layer_input.reshape(tok, width)
    y = output_grad.reshape(tok, width)
    first, second = weight_in[0], weight_out[0]
    pairs = functools.partial(exchange_pairs, me=index, count=count)

    *send, hit_mine, hit_other, gates, key = prep(
        me, expert_lists[0], gate_values[0], x, y, group
    )
    slots = send[0].shape[1] // 2
    half = group * slots
    single = functools.partial(exchange_single, me=index, count=count)
    got_near = single(send[:group], 0)
    got_far = single(send[group:], group)
    more, early = {}, got_far[::2]
    if count == 8:
        split = group // 2
        away, close = exchange_apart(send[group + split], group + split, count)
        got_far[split], more[split] = (away, 0), (close, 0)
        early = [got_far[0], got_far[split]]

    probs, turned = probabilities(query_rows, key_rows, after=[hit_mine])
    rows_near, rest_near = expert(
        got_near, gates[:half], first, second, after=[turned, *arrays(early)]
    )
    back_near = single(rows_near, 0)
    late = arrays(got_far[1::2]) + arrays(more.values())
    send_near = combine(me, hit_mine, back_near, y, count, after=late)
    grad_near = pairs(send_near)
    rows_far, rest_far = expert(
        got_far, gates[half:], first, second, more=more, after=send_near[:1]
    )
    back_far = single(rows_far, 0)

    x_near, scaled_near, act_near, pre_near, sums_near = rest_near
    x_far, scaled_far, act_far, pre_far, sums_far = rest_far
    crossed = grad_near[1:]
    in_term = weight_gradient((x_near, pre_near), (x_far, pre_far), False, after=crossed)
    *send_far, in_term = combine(me, hit_other, back_far, None, count, carry=in_term)
    in_share = lax.psum_scatter(in_term, "slab", scatter_dimension=0, tiled=True).astype(F32)
    grad_far = pairs(send_far)
    out_term = weight_gradient(
        (scaled_near, act_near), (scaled_far, act_far), True, after=send_far[:1]
    )
    slot_sums = jnp.concatenate([sums_near, sums_far]).reshape(count, slots, 1)
    slot_ids = jnp.arange(slots, dtype=jnp.int32)[None, :, None]
    gate_grad = jnp.sum(jnp.where(key[:, None, :] == slot_ids, slot_sums, 0.0), axis=(0, 1))

    odd, out_term = meet(grad_near, grad_far, out_term)
    out_share = lax.psum_scatter(out_term, "slab", scatter_dimension=0, tiled=True).astype(F32)
    odd = other_core(odd, count)
    value_send, grad_attn = value_gradient(me, turned, odd, grad_near, grad_far, count)
    pair_send = pair_gradients(me, probs, grad_attn, query_rows, key_rows, value_rows, count)
    (value_grad,) = place(me, single(value_send, 0), after=pair_send[:1])
    query_grad, key_grad = place(me, single(pair_send, 0), after=[in_share])
    whole = (frames_here, patches, width)
    return (
        gate_grad.reshape(1, 1, cap),
        in_share[None],
        out_share[None],
        query_grad.reshape(whole),
        key_grad.reshape(whole),
        value_grad.reshape(whole),
    )


def solution(mesh):
    return jax.shard_map(
        body,
        mesh=mesh,
        in_specs=(
            P("dev", "slab", None),
            P("dev", "slab", None),
            P("slab", None, None),
            P("slab", "dev", None),
            P("dev", None, None),
            P("dev", None, None),
            P(None, ("slab", "dev"), None),
            P(None, ("slab", "dev"), None),
            P(None, ("slab", "dev"), None),
        ),
        out_specs=(
            P("slab", "dev", None),
            P("dev", "slab", None),
            P("dev", "slab", None),
            P("dev", "slab", None),
            P("dev", "slab", None),
            P("dev", "slab", None),
        ),
        check_vma=False,
    )
```

```python
import functools

import jax
import jax.numpy as jnp
from jax import lax
from jax.experimental import pallas as pl
from jax.experimental.pallas import tpu as pltpu
from jax.sharding import PartitionSpec as P

HEADS = 16
LANES = 128
ROOT = 0.7978845608028654
CUBE = 0.044715
BF = jnp.bfloat16
F32 = jnp.float32
VMEM_LIMIT = 56 * 1024 * 1024

ROWS_COLS = (((1,), (0,)), ((), ()))
LAST_LAST = (((1,), (1,)), ((), ()))
FIRST_FIRST = (((0,), (0,)), ((), ()))


def dot(left, right, dims=ROWS_COLS):
    return lax.dot_general(left, right, dims, preferred_element_type=F32)


def call(kernel, out_shape, in_specs, args, out_specs, after=(), carry=None, flops=0, nbytes=0, **kwargs):
    held = list(after) if carry is None else [*after, carry]
    skip = len(args)
    aliases = {}
    if carry is not None:
        aliases = {skip + len(held) - 1: len(out_shape)}
        out_shape = [*out_shape, jax.ShapeDtypeStruct(carry.shape, carry.dtype)]
        out_specs = [*out_specs, ANY]

    def run(*refs):
        refs = [*refs[:skip], *refs[skip + len(held) :]]
        if carry is not None:
            del refs[skip + len(out_shape) - 1]
        kernel(*refs)

    return pl.pallas_call(
        run,
        out_shape=out_shape,
        in_specs=list(in_specs) + [ANY] * len(held),
        out_specs=out_specs,
        input_output_aliases=aliases,
        compiler_params=pltpu.CompilerParams(vmem_limit_bytes=VMEM_LIMIT),
        cost_estimate=pl.CostEstimate(flops=flops, bytes_accessed=nbytes, transcendentals=0),
        **kwargs,
    )(*args, *held)


ANY = pl.BlockSpec(memory_space=pl.ANY)
SMEM = pl.BlockSpec(memory_space=pltpu.SMEM)
WHOLE = pl.BlockSpec(memory_space=pltpu.VMEM)


def shape(dims, dtype=BF):
    return jax.ShapeDtypeStruct(dims, dtype)


def exchange_all(blocks, which, me, count):
    size = len(which)
    first = which[0]
    order = me ^ first
    groups = None
    if size < count:
        groups = [[g * size + j for j in range(size)] for g in range(count // size)]
    places = (order % size) ^ jnp.arange(size, dtype=jnp.int32)
    stacked = jnp.stack(blocks)[places]
    if first:
        across = [(i, i ^ first) for i in range(count)]
        stacked = lax.ppermute(stacked, "dev", across)
        places = (me % size) ^ jnp.arange(size, dtype=jnp.int32)
    got = lax.all_to_all(stacked, "dev", 0, 0, axis_index_groups=groups, tiled=True)[places]
    return [got[i] for i in range(size)]


def exchange_pairs(pairs, me, count):
    if count > 8:
        blocks = exchange_all([pair[j] for pair in pairs for j in range(2)], list(range(count)), me, count)
        mates = other_core(jnp.stack(blocks[1::2]), count)
        return [jnp.stack([block, mates[i]]) for i, block in enumerate(blocks[::2])]
    return [
        lax.ppermute(pair, "dev", [(d, d ^ (2 * i)) for d in range(count)]) if i else pair
        for i, pair in enumerate(pairs)
    ]


def other_core(array, count):
    return lax.ppermute(array, "dev", [(d, d ^ 1) for d in range(count)])


def exchange_single(blocks, first, me, count):
    which = list(range(first, first + len(blocks)))
    if count > 8:
        got = exchange_all([b[0] for b in blocks], which, me, count)
        return [(block[None], 0) for block in got]
    pairs = {k: [(d, d ^ k) for d in range(count)] for k in which}
    return [(lax.ppermute(b, "dev", pairs[k]) if k else b, 0) for b, k in zip(blocks, which)]


def exchange_apart(block, k, count):
    pairs = [(d, d ^ k) for d in range(count)]
    far = [(d, e) for d, e in pairs if abs(d - e) > count // 2]
    near = [(d, e) for d, e in pairs if abs(d - e) <= count // 2]
    return lax.ppermute(block, "dev", far), lax.ppermute(block, "dev", near)


def arrays(got):
    return [array for array, _ in got]


def block_specs(got, block, index_map):
    return [
        pl.BlockSpec((None, *block), lambda *i, at=at: (at, *index_map(*i))) for _, at in got
    ]


def prep_kernel(count, group, slots, tok, me_ref, table_ref, gate_ref, x_ref, y_ref, *refs):
    send_refs = refs[:count]
    mine_ref, other_ref, gate_out, key_out, rank_ref = refs[count:]
    me = me_ref[0]
    cap = table_ref.shape[1]
    width = table_ref.shape[0]
    upper = lax.broadcasted_iota(jnp.int32, (cap, cap), 0) < lax.broadcasted_iota(
        jnp.int32, (cap, cap), 1
    )
    upper = upper.astype(F32).astype(BF)
    table = table_ref[...]
    slot_ids = lax.broadcasted_iota(jnp.int32, (slots, cap), 0)
    tok_ids = lax.broadcasted_iota(jnp.int32, (slots, tok), 1)

    def ranked(inside):
        rank = dot(inside.astype(F32).astype(BF), upper).astype(jnp.int32)
        return jnp.where(inside, rank, -1)

    def hits(frame, ks, out_ref):
        low = frame * tok
        rank_ref[...] = ranked((table >= low) & (table < low + tok))
        for place, k in enumerate(ks):
            row = rank_ref[pl.ds(me ^ k, 1), :]
            offset = table_ref[pl.ds(me ^ k, 1), :] - low
            found = jnp.where(row == slot_ids, (offset + 1).astype(F32), 0.0)
            column = (jnp.sum(found, axis=1, keepdims=True) - 1.0).astype(jnp.int32)
            out_ref[place * slots : (place + 1) * slots, :] = (
                (column == tok_ids).astype(F32).astype(BF)
            )

    hits(me, range(count), mine_ref)
    for half, source in enumerate((x_ref, y_ref)):
        rows = dot(mine_ref[...], source[...]).astype(BF)
        for k in range(count):
            send_refs[k][0, half * slots : (half + 1) * slots, :] = rows[
                k * slots : (k + 1) * slots
            ]
    hits(me ^ group, range(group), other_ref)

    mine_row = table_ref[pl.ds(me, 1), :]
    frames = (lax.broadcasted_iota(jnp.int32, (width, cap), 0) ^ me) * tok
    key = ranked((mine_row >= frames) & (mine_row < frames + tok))
    key_out[...] = key
    for k in range(count):
        found = jnp.where(key[k : k + 1, :] == slot_ids, gate_ref[...], 0.0)
        gate_out[k * slots : (k + 1) * slots, :] = jnp.sum(found, axis=1, keepdims=True)


def prep(me, table, gate_row, x, y, group):
    count, cap = table.shape
    tok, width = x.shape
    slots = 2 * cap // count
    return call(
        functools.partial(prep_kernel, count, group, slots, tok),
        [shape((1, 2 * slots, width))] * count
        + [
            shape((count * slots, tok)),
            shape((group * slots, tok)),
            shape((count * slots, 1), F32),
            shape((count, cap), jnp.int32),
        ],
        [SMEM, WHOLE, WHOLE, WHOLE, WHOLE],
        [me, table, gate_row, x, y],
        flops=4 * count * slots * tok * width,
        nbytes=8 * count * slots * width,
        out_specs=[WHOLE] * (count + 4),
        scratch_shapes=[pltpu.VMEM((count, cap), jnp.int32)],
        name="prep",
    )


def expert_kernel(parts, steps, apart, gate_ref, first_ref, second_ref, *refs):
    in_refs = refs[:parts]
    more_refs = dict(zip(apart, refs[parts:]))
    outs = refs[parts + len(apart) :]
    row_refs = outs[:parts]
    x_all, scaled, act_ref, pre_ref, gg_ref, y_all, total = outs[parts:]
    step = pl.program_id(0)
    slots = in_refs[0].shape[0] // 2

    @pl.when(step == 0)
    def _():
        for k in range(parts):
            place = slice(k * slots, (k + 1) * slots)
            value = in_refs[k][...]
            if k in more_refs:
                value = value + more_refs[k][...]
            x_all[place, :] = value[:slots, :]
            y_rows = value[slots:, :]
            y_all[place, :] = y_rows
            scaled[place, :] = (gate_ref[place, :] * y_rows.astype(F32)).astype(BF)
        gg_ref[...] = jnp.zeros_like(gg_ref)
        total[...] = jnp.zeros_like(total)

    first = first_ref[...]
    second = second_ref[...]
    u = dot(x_all[...], first)
    back = dot(y_all[...], second, LAST_LAST)
    square = u * u
    t = jnp.tanh(u * (ROOT + (ROOT * CUBE) * square))
    half = 0.5 + 0.5 * t
    act = (u * half).astype(BF)
    slope = half + u * (1.0 - t * t) * (0.5 * ROOT + (1.5 * ROOT * CUBE) * square)
    act_ref[...] = act
    gg_ref[...] += jnp.sum(act.astype(F32) * back, axis=1, keepdims=True)
    pre = (gate_ref[...] * back * slope).astype(BF)
    pre_ref[...] = pre
    total[...] += dot(pre, first, LAST_LAST)

    @pl.when(step == steps - 1)
    def _():
        for k in range(parts):
            row_refs[k][0] = total[k * slots : (k + 1) * slots, :].astype(BF)


def expert(blocks, gates, weight_in, weight_out, more=(), after=()):
    more = dict(more)
    parts = len(blocks)
    _, slots, width = blocks[0][0].shape
    slots //= 2
    rows = parts * slots
    hidden = weight_in.shape[1]
    tile = 768 if hidden % 768 == 0 else hidden
    steps = hidden // tile
    fixed = lambda dims: pl.BlockSpec(dims, lambda i: (0, 0))
    outs = call(
        functools.partial(expert_kernel, parts, steps, tuple(more)),
        [shape((1, slots, width))] * parts
        + [
            shape((rows, width)),
            shape((rows, width)),
            shape((rows, hidden)),
            shape((rows, hidden)),
            shape((rows, 1), F32),
        ],
        [
            fixed((rows, 1)),
            pl.BlockSpec((width, tile), lambda i: (0, i)),
            pl.BlockSpec((tile, width), lambda i: (i, 0)),
        ]
        + block_specs([*blocks, *more.values()], (2 * slots, width), lambda i: (0, 0)),
        [gates, weight_in, weight_out, *arrays(blocks), *arrays(more.values())],
        flops=6 * rows * width * hidden,
        nbytes=4 * width * hidden + 4 * rows * hidden + 8 * rows * width,
        after=after,
        grid=(steps,),
        out_specs=[pl.BlockSpec((1, slots, width), lambda i: (0, 0, 0))] * parts
        + [
            fixed((rows, width)),
            fixed((rows, width)),
            pl.BlockSpec((rows, tile), lambda i: (0, i)),
            pl.BlockSpec((rows, tile), lambda i: (0, i)),
            fixed((rows, 1)),
        ],
        scratch_shapes=[pltpu.VMEM((rows, width), BF), pltpu.VMEM((rows, width), F32)],
        name="expert",
    )
    return outs[:parts], outs[parts:]


def weight_kernel(turn, near_left, near_right, far_left, far_right, out_ref):
    left, right = (near_left, far_left), (near_right, far_right)
    value = sum(dot(a[...], b[...], FIRST_FIRST) for a, b in zip(left, right))
    out_ref[...] = value.astype(BF)


def weight_gradient(near, far, hidden_first, after=()):
    width, hidden = near[0].shape[1], near[1].shape[1]
    tile = 768 if hidden % 768 == 0 else hidden
    args, specs = [], []
    for rows, units in (near, far):
        all_rows = pl.BlockSpec(rows.shape, lambda i: (0, 0))
        some = pl.BlockSpec((units.shape[0], tile), lambda i: (0, i))
        args += [units, rows] if hidden_first else [rows, units]
        specs += [some, all_rows] if hidden_first else [all_rows, some]
    out, out_spec = (width, hidden), pl.BlockSpec((width, tile), lambda i: (0, i))
    if hidden_first:
        out, out_spec = (hidden, width), pl.BlockSpec((tile, width), lambda i: (i, 0))
    return call(
        functools.partial(weight_kernel, hidden_first),
        shape(out),
        specs,
        args,
        flops=4 * near[0].shape[0] * width * hidden,
        nbytes=2 * width * hidden,
        after=after,
        grid=(hidden // tile,),
        out_specs=out_spec,
        name="weight_gradient",
    )


def combine_kernel(count, parts, plus, me_ref, hit_ref, *refs):
    rows = jnp.concatenate([ref[...] for ref in refs[:parts]], axis=0)
    refs = refs[parts:]
    if plus:
        y_ref, refs = refs[0], refs[1:]
    outs, total = refs[: count // 2], refs[count // 2]
    total[...] = dot(hit_ref[...], rows, FIRST_FIRST)
    piece = outs[0].shape[1]
    for k in range(count):
        place = pl.ds(pl.multiple_of((me_ref[0] ^ k) * piece, piece), piece)
        value = total[place, :]
        if plus:
            value = value + y_ref[place, :].astype(F32)
        outs[k // 2][k % 2] = value.astype(BF)


def combine(me, hit, blocks, y, count, after=(), carry=None):
    parts = len(blocks)
    _, slots, width = blocks[0][0].shape
    tok = hit.shape[1]
    plus = [] if y is None else [y]
    rows = parts * slots
    return call(
        functools.partial(combine_kernel, count, parts, bool(plus)),
        [shape((2, tok // count, width))] * (count // 2),
        [SMEM, pl.BlockSpec((rows, tok), lambda i: (0, 0))]
        + block_specs(blocks, (slots, width), lambda i: (0, 0))
        + [pl.BlockSpec(b.shape, lambda i: (0, 0)) for b in plus],
        [me, hit, *arrays(blocks), *plus],
        flops=2 * rows * tok * width,
        nbytes=6 * tok * width,
        after=after,
        carry=carry,
        grid=(1,),
        out_specs=[pl.BlockSpec((2, tok // count, width), lambda i: (0, 0, 0))] * (count // 2),
        scratch_shapes=[pltpu.VMEM((tok, width), F32)],
        name="combine",
    )


def windows(width):
    size = width // HEADS
    for head in range(HEADS):
        start, stop = head * size, (head + 1) * size
        low, high = start // LANES, -(-stop // LANES)
        yield head, start, stop, low, high, slice(low * LANES, min(high * LANES, width))


def head_lanes(start, stop, window):
    lane = lax.broadcasted_iota(jnp.int32, (1, window.stop - window.start), 1) + window.start
    return (lane >= start) & (lane < stop)


def keep(held, part, inside, low, high):
    for tile in range(low, high):
        lanes = slice((tile - low) * LANES, min((tile - low + 1) * LANES, part.shape[1]))
        new = part[:, lanes]
        if held[tile] is not None:
            new = jnp.where(inside[:, lanes], new, held[tile])
        held[tile] = new


def probs_kernel(q_ref, k_ref, probs_ref, turned_ref):
    frames, patches, width = q_ref.shape
    rows = frames * patches
    scale = (width // HEADS) ** -0.5
    query = q_ref[...].reshape(rows, width)
    keys = k_ref[...].reshape(rows, width)
    same = (lax.broadcasted_iota(jnp.int32, (rows, rows), 0) % patches) == (
        lax.broadcasted_iota(jnp.int32, (rows, rows), 1) % patches
    )
    for head, start, stop, low, high, window in windows(width):
        inside = head_lanes(start, stop, window)
        q_win = jnp.where(inside, query[:, window], jnp.zeros((), BF))
        scores = jnp.where(same, dot(q_win, keys[:, window], LAST_LAST) * scale, -1e30)
        probs = jnp.exp(scores - jnp.max(scores, axis=1, keepdims=True))
        probs = probs / jnp.sum(probs, axis=1, keepdims=True)
        probs_ref[0, head] = probs
        turned_ref[0, head] = probs.T.astype(BF)


def patch_tile(frames, patches):
    return 16 if patches % 16 == 0 else patches


def probabilities(query, keys, after=()):
    frames, patches, width = query.shape
    tile = patch_tile(frames, patches)
    steps = patches // tile
    rows = frames * tile
    wide = pl.BlockSpec((frames, tile, width), lambda i: (0, i, 0))
    square = pl.BlockSpec((1, HEADS, rows, rows), lambda i: (i, 0, 0, 0))
    return call(
        probs_kernel,
        [shape((steps, HEADS, rows, rows), F32), shape((steps, HEADS, rows, rows))],
        [wide, wide],
        [query, keys],
        flops=8 * frames * patches * rows * width,
        nbytes=4 * frames * patches * width + 6 * steps * HEADS * rows * rows,
        after=after,
        grid=(steps,),
        out_specs=[square, square],
        name="probs",
    )


def meet_kernel(chips, *refs):
    near, far, out_ref = refs[:chips], refs[chips : 2 * chips], refs[2 * chips]
    for i in range(chips):
        value = near[i][...].astype(F32) + far[i ^ (chips // 2)][...].astype(F32)
        out_ref[i] = value.astype(BF)


def meet(near, far, carry):
    chips = len(near)
    _, piece, width = near[0].shape
    spec = pl.BlockSpec((None, piece, width), lambda i: (1, 0, 0))
    return call(
        functools.partial(meet_kernel, chips),
        [shape((chips, piece, width))],
        [spec] * (2 * chips),
        [*near, *far],
        nbytes=6 * chips * piece * width,
        carry=carry,
        grid=(1,),
        out_specs=[pl.BlockSpec((chips, piece, width), lambda i: (0, 0, 0))],
        name="meet",
    )


def value_kernel(count, me_ref, turned_ref, odd_ref, *refs):
    chips = count // 2
    near, far, refs = refs[:chips], refs[chips : 2 * chips], refs[2 * chips :]
    outs = refs[:count]
    grad_ref, result = refs[count:]
    me = me_ref[0]
    frames, patches, width = grad_ref.shape
    rows = frames * patches
    for i in range(chips):
        value = near[i][...].astype(F32) + far[i ^ (chips // 2)][...].astype(F32)
        grad_ref[me ^ (2 * i)] = value.astype(BF)
        grad_ref[me ^ (2 * i + 1)] = odd_ref[i]
    grad = grad_ref[...].reshape(rows, width)
    held = [None] * -(-width // LANES)
    for head, start, stop, low, high, window in windows(width):
        inside = head_lanes(start, stop, window)
        keep(held, dot(turned_ref[0, head], grad[:, window]), inside, low, high)
    for tile, value in enumerate(held):
        lanes = slice(tile * LANES, tile * LANES + value.shape[1])
        result[:, :, lanes] = value.astype(BF).reshape(frames, patches, value.shape[1])
    for k in range(count):
        outs[k][0] = result[me ^ k]


def value_gradient(me, turned, odd, near, far, count, after=()):
    _, piece, width = near[0].shape
    steps, _, rows, _ = turned.shape
    tile = piece // steps
    frames = rows // tile
    wide = pl.BlockSpec((frames, tile, width), lambda i: (0, i, 0))
    even = pl.BlockSpec((None, tile, width), lambda i: (0, i, 0))
    outs = call(
        functools.partial(value_kernel, count),
        [shape((1, piece, width))] * count + [shape((frames, piece, width))],
        [
            SMEM,
            pl.BlockSpec((1, HEADS, rows, rows), lambda i: (i, 0, 0, 0)),
            pl.BlockSpec((count // 2, tile, width), lambda i: (0, i, 0)),
        ]
        + [even] * (2 * len(near)),
        [me, turned, odd, *near, *far],
        flops=4 * frames * piece * rows * width,
        nbytes=8 * frames * piece * width,
        after=after,
        grid=(steps,),
        out_specs=[pl.BlockSpec((1, tile, width), lambda i: (0, i, 0))] * count + [wide],
        scratch_shapes=[pltpu.VMEM((frames, tile, width), BF)],
        name="value_gradient",
    )
    return outs[:count], outs[count]


def pair_kernel(count, me_ref, probs_ref, grad_ref, q_ref, k_ref, v_ref, *refs):
    outs, result = refs[:count], refs[count]
    me = me_ref[0]
    frames, patches, width = q_ref.shape
    rows = frames * patches
    scale = (width // HEADS) ** -0.5
    query, keys, values, grad = (
        ref[...].reshape(rows, width) for ref in (q_ref, k_ref, v_ref, grad_ref)
    )
    tiles = -(-width // LANES)
    held = [[None] * tiles for _ in range(2)]
    for head, start, stop, low, high, window in windows(width):
        inside = head_lanes(start, stop, window)
        g_win = jnp.where(inside, grad[:, window], jnp.zeros((), BF))
        prob_grad = dot(g_win, values[:, window], LAST_LAST)
        probs = probs_ref[0, head]
        delta = jnp.sum(probs * prob_grad, axis=1, keepdims=True)
        score_grad = (probs * (prob_grad - delta)).astype(BF)
        keep(held[0], dot(score_grad, keys[:, window]) * scale, inside, low, high)
        keep(held[1], dot(score_grad, query[:, window], FIRST_FIRST) * scale, inside, low, high)
    for which in range(2):
        for tile, value in enumerate(held[which]):
            lanes = slice(tile * LANES, tile * LANES + value.shape[1])
            value = value.astype(BF).reshape(frames, patches, value.shape[1])
            result[which, :, :, lanes] = value
    for k in range(count):
        for which in range(2):
            outs[k][0, which] = result[which, me ^ k]


def pair_gradients(me, probs, grad, query, keys, values, count, after=()):
    frames, piece, width = query.shape
    steps, _, rows, _ = probs.shape
    tile = piece // steps
    wide = pl.BlockSpec((frames, tile, width), lambda i: (0, i, 0))
    return call(
        functools.partial(pair_kernel, count),
        [shape((1, 2, piece, width))] * count,
        [SMEM, pl.BlockSpec((1, HEADS, rows, rows), lambda i: (i, 0, 0, 0))] + [wide] * 4,
        [me, probs, grad, query, keys, values],
        flops=12 * frames * piece * rows * width,
        nbytes=16 * frames * piece * width,
        after=after,
        grid=(steps,),
        out_specs=[pl.BlockSpec((1, 2, tile, width), lambda i: (0, 0, i, 0))] * count,
        scratch_shapes=[pltpu.VMEM((2, frames, tile, width), BF)],
        name="pair_gradients",
    )


def spread(count):
    half, quarter = count // 2, count // 4
    far = [k for i in range(quarter) for k in (half + quarter + i, half + i)]
    return far + list(range(half - 1, -1, -1))


def place_kernel(order, outs_count, me_ref, *refs):
    blocks, outs = refs[: len(order)], refs[len(order) :]
    piece = blocks[0].shape[-2]
    for k, block in zip(order, blocks):
        place = pl.ds(pl.multiple_of((me_ref[0] ^ k) * piece, piece), piece)
        if outs_count == 1:
            outs[0][place, :] = block[...]
        else:
            for which in range(outs_count):
                outs[which][place, :] = block[which]


def place(me, blocks, after=()):
    count = len(blocks)
    dims = blocks[0][0].shape[1:]
    tok = count * dims[-2]
    outs_count = dims[0] if len(dims) == 3 else 1
    order = spread(count)
    blocks = [blocks[k] for k in order]
    return call(
        functools.partial(place_kernel, order, outs_count),
        [shape((tok, dims[-1]))] * outs_count,
        [SMEM] + block_specs(blocks, dims, lambda i: (0,) * len(dims)),
        [me, *arrays(blocks)],
        nbytes=4 * outs_count * tok * dims[-1],
        after=after,
        grid=(1,),
        out_specs=[pl.BlockSpec((tok, dims[-1]), lambda i: (0, 0))] * outs_count,
        name="place",
    )


def body(
    layer_input,
    output_grad,
    expert_lists,
    gate_values,
    weight_in,
    weight_out,
    query_rows,
    key_rows,
    value_rows,
):
    count = lax.axis_size("dev")
    index = lax.axis_index("dev").astype(jnp.int32)
    me = index.reshape(1)
    frames_here, patches, width = layer_input.shape
    tok = frames_here * patches
    cap = expert_lists.shape[2]
    group = count // 2
    x = layer_input.reshape(tok, width)
    y = output_grad.reshape(tok, width)
    first, second = weight_in[0], weight_out[0]
    pairs = functools.partial(exchange_pairs, me=index, count=count)

    *send, hit_mine, hit_other, gates, key = prep(
        me, expert_lists[0], gate_values[0], x, y, group
    )
    slots = send[0].shape[1] // 2
    half = group * slots
    single = functools.partial(exchange_single, me=index, count=count)
    got_near = single(send[:group], 0)
    got_far = single(send[group:], group)
    more, early = {}, got_far[::2]
    if count == 8:
        split = group // 2
        away, close = exchange_apart(send[group + split], group + split, count)
        got_far[split], more[split] = (away, 0), (close, 0)
        early = [got_far[0], got_far[split]]

    probs, turned = probabilities(query_rows, key_rows, after=[hit_mine])
    rows_near, rest_near = expert(
        got_near, gates[:half], first, second, after=[turned, *arrays(early)]
    )
    back_near = single(rows_near, 0)
    late = arrays(got_far[1::2]) + arrays(more.values())
    send_near = combine(me, hit_mine, back_near, y, count, after=late)
    grad_near = pairs(send_near)
    rows_far, rest_far = expert(
        got_far, gates[half:], first, second, more=more, after=send_near[:1]
    )
    back_far = single(rows_far, 0)

    x_near, scaled_near, act_near, pre_near, sums_near = rest_near
    x_far, scaled_far, act_far, pre_far, sums_far = rest_far
    crossed = grad_near[2:]
    in_term = weight_gradient((x_near, pre_near), (x_far, pre_far), False)
    *send_far, in_term = combine(
        me, hit_other, back_far, None, count, after=crossed, carry=in_term
    )
    in_share = lax.psum_scatter(in_term, "slab", scatter_dimension=0, tiled=True).astype(F32)
    grad_far = pairs(send_far)
    out_term = weight_gradient(
        (scaled_near, act_near), (scaled_far, act_far), True, after=send_far[:1]
    )
    slot_sums = jnp.concatenate([sums_near, sums_far]).reshape(count, slots, 1)
    slot_ids = jnp.arange(slots, dtype=jnp.int32)[None, :, None]
    gate_grad = jnp.sum(jnp.where(key[:, None, :] == slot_ids, slot_sums, 0.0), axis=(0, 1))

    odd, out_term = meet(grad_near, grad_far, out_term)
    out_share = lax.psum_scatter(out_term, "slab", scatter_dimension=0, tiled=True).astype(F32)
    odd = other_core(odd, count)
    value_send, grad_attn = value_gradient(me, turned, odd, grad_near, grad_far, count)
    pair_send = pair_gradients(me, probs, grad_attn, query_rows, key_rows, value_rows, count)
    (value_grad,) = place(me, single(value_send, 0), after=pair_send[:1])
    query_grad, key_grad = place(me, single(pair_send, 0), after=[in_share])
    whole = (frames_here, patches, width)
    return (
        gate_grad.reshape(1, 1, cap),
        in_share[None],
        out_share[None],
        query_grad.reshape(whole),
        key_grad.reshape(whole),
        value_grad.reshape(whole),
    )


def solution(mesh):
    return jax.shard_map(
        body,
        mesh=mesh,
        in_specs=(
            P("dev", "slab", None),
            P("dev", "slab", None),
            P("slab", None, None),
            P("slab", "dev", None),
            P("dev", None, None),
            P("dev", None, None),
            P(None, ("slab", "dev"), None),
            P(None, ("slab", "dev"), None),
            P(None, ("slab", "dev"), None),
        ),
        out_specs=(
            P("slab", "dev", None),
            P("dev", "slab", None),
            P("dev", "slab", None),
            P("dev", "slab", None),
            P("dev", "slab", None),
            P("dev", "slab", None),
        ),
        check_vma=False,
    )
```

```python
import functools

import jax
import jax.numpy as jnp
from jax import lax
from jax.experimental import pallas as pl
from jax.experimental.pallas import tpu as pltpu
from jax.sharding import PartitionSpec as P

HEADS = 16
LANES = 128
ROOT = 0.7978845608028654
CUBE = 0.044715
BF = jnp.bfloat16
F32 = jnp.float32
VMEM_LIMIT = 56 * 1024 * 1024

ROWS_COLS = (((1,), (0,)), ((), ()))
LAST_LAST = (((1,), (1,)), ((), ()))
FIRST_FIRST = (((0,), (0,)), ((), ()))


def dot(left, right, dims=ROWS_COLS):
    return lax.dot_general(left, right, dims, preferred_element_type=F32)


def call(kernel, out_shape, in_specs, args, out_specs, after=(), carry=None, flops=0, nbytes=0, **kwargs):
    held = list(after) if carry is None else [*after, carry]
    skip = len(args)
    aliases = {}
    if carry is not None:
        aliases = {skip + len(held) - 1: len(out_shape)}
        out_shape = [*out_shape, jax.ShapeDtypeStruct(carry.shape, carry.dtype)]
        out_specs = [*out_specs, ANY]

    def run(*refs):
        refs = [*refs[:skip], *refs[skip + len(held) :]]
        if carry is not None:
            del refs[skip + len(out_shape) - 1]
        kernel(*refs)

    return pl.pallas_call(
        run,
        out_shape=out_shape,
        in_specs=list(in_specs) + [ANY] * len(held),
        out_specs=out_specs,
        input_output_aliases=aliases,
        compiler_params=pltpu.CompilerParams(vmem_limit_bytes=VMEM_LIMIT),
        cost_estimate=pl.CostEstimate(flops=flops, bytes_accessed=nbytes, transcendentals=0),
        **kwargs,
    )(*args, *held)


ANY = pl.BlockSpec(memory_space=pl.ANY)
SMEM = pl.BlockSpec(memory_space=pltpu.SMEM)
WHOLE = pl.BlockSpec(memory_space=pltpu.VMEM)


def shape(dims, dtype=BF):
    return jax.ShapeDtypeStruct(dims, dtype)


def exchange_all(blocks, which, me, count):
    size = len(which)
    first = which[0]
    order = me ^ first
    groups = None
    if size < count:
        groups = [[g * size + j for j in range(size)] for g in range(count // size)]
    places = (order % size) ^ jnp.arange(size, dtype=jnp.int32)
    stacked = jnp.stack(blocks)[places]
    if first:
        across = [(i, i ^ first) for i in range(count)]
        stacked = lax.ppermute(stacked, "dev", across)
        places = (me % size) ^ jnp.arange(size, dtype=jnp.int32)
    got = lax.all_to_all(stacked, "dev", 0, 0, axis_index_groups=groups, tiled=True)[places]
    return [got[i] for i in range(size)]


def exchange_pairs(pairs, me, count):
    if count > 8:
        blocks = exchange_all([pair[j] for pair in pairs for j in range(2)], list(range(count)), me, count)
        mates = other_core(jnp.stack(blocks[1::2]), count)
        return [jnp.stack([block, mates[i]]) for i, block in enumerate(blocks[::2])]
    return [
        lax.ppermute(pair, "dev", [(d, d ^ (2 * i)) for d in range(count)]) if i else pair
        for i, pair in enumerate(pairs)
    ]


def other_core(array, count):
    return lax.ppermute(array, "dev", [(d, d ^ 1) for d in range(count)])


def exchange_single(blocks, first, me, count):
    which = list(range(first, first + len(blocks)))
    if count > 8:
        got = exchange_all([b[0] for b in blocks], which, me, count)
        return [(block[None], 0) for block in got]
    pairs = {k: [(d, d ^ k) for d in range(count)] for k in which}
    return [(lax.ppermute(b, "dev", pairs[k]) if k else b, 0) for b, k in zip(blocks, which)]


def exchange_apart(block, k, count):
    pairs = [(d, d ^ k) for d in range(count)]
    far = [(d, e) for d, e in pairs if abs(d - e) > count // 2]
    near = [(d, e) for d, e in pairs if abs(d - e) <= count // 2]
    return lax.ppermute(block, "dev", far), lax.ppermute(block, "dev", near)


def arrays(got):
    return [array for array, _ in got]


def block_specs(got, block, index_map):
    return [
        pl.BlockSpec((None, *block), lambda *i, at=at: (at, *index_map(*i))) for _, at in got
    ]


def prep_kernel(count, group, slots, tok, me_ref, table_ref, gate_ref, x_ref, y_ref, *refs):
    send_refs = refs[:count]
    mine_ref, other_ref, gate_out, key_out, rank_ref = refs[count:]
    me = me_ref[0]
    cap = table_ref.shape[1]
    width = table_ref.shape[0]
    upper = lax.broadcasted_iota(jnp.int32, (cap, cap), 0) < lax.broadcasted_iota(
        jnp.int32, (cap, cap), 1
    )
    upper = upper.astype(F32).astype(BF)
    table = table_ref[...]
    slot_ids = lax.broadcasted_iota(jnp.int32, (slots, cap), 0)
    tok_ids = lax.broadcasted_iota(jnp.int32, (slots, tok), 1)

    def ranked(inside):
        rank = dot(inside.astype(F32).astype(BF), upper).astype(jnp.int32)
        return jnp.where(inside, rank, -1)

    def hits(frame, ks, out_ref):
        low = frame * tok
        rank_ref[...] = ranked((table >= low) & (table < low + tok))
        for place, k in enumerate(ks):
            row = rank_ref[pl.ds(me ^ k, 1), :]
            offset = table_ref[pl.ds(me ^ k, 1), :] - low
            found = jnp.where(row == slot_ids, (offset + 1).astype(F32), 0.0)
            column = (jnp.sum(found, axis=1, keepdims=True) - 1.0).astype(jnp.int32)
            out_ref[place * slots : (place + 1) * slots, :] = (
                (column == tok_ids).astype(F32).astype(BF)
            )

    def send(source):
        rows = dot(mine_ref[...], source[...]).astype(BF)
        for k in range(count):
            send_refs[k][0] = rows[k * slots : (k + 1) * slots]

    @pl.when(pl.program_id(0) == 0)
    def _():
        hits(me, range(count), mine_ref)
        send(x_ref)

    @pl.when(pl.program_id(0) == 1)
    def _():
        send(y_ref)
        hits(me ^ group, range(group), other_ref)
        mine_row = table_ref[pl.ds(me, 1), :]
        frames = (lax.broadcasted_iota(jnp.int32, (width, cap), 0) ^ me) * tok
        key = ranked((mine_row >= frames) & (mine_row < frames + tok))
        key_out[...] = key
        for k in range(count):
            found = jnp.where(key[k : k + 1, :] == slot_ids, gate_ref[...], 0.0)
            gate_out[k * slots : (k + 1) * slots, :] = jnp.sum(found, axis=1, keepdims=True)


def prep(me, table, gate_row, x, y, group):
    count, cap = table.shape
    tok, width = x.shape
    slots = 2 * cap // count
    return call(
        functools.partial(prep_kernel, count, group, slots, tok),
        [shape((1, 2 * slots, width))] * count
        + [
            shape((count * slots, tok)),
            shape((group * slots, tok)),
            shape((count * slots, 1), F32),
            shape((count, cap), jnp.int32),
        ],
        [SMEM]
        + [pl.BlockSpec(a.shape, lambda i: (0, 0)) for a in (table, gate_row, x, y)],
        [me, table, gate_row, x, y],
        flops=4 * count * slots * tok * width,
        nbytes=8 * count * slots * width,
        grid=(2,),
        out_specs=[pl.BlockSpec((1, slots, width), lambda i: (0, i, 0))] * count
        + [
            pl.BlockSpec((count * slots, tok), lambda i: (0, 0)),
            pl.BlockSpec((group * slots, tok), lambda i: (0, 0)),
            pl.BlockSpec((count * slots, 1), lambda i: (0, 0)),
            pl.BlockSpec((count, cap), lambda i: (0, 0)),
        ],
        scratch_shapes=[pltpu.VMEM((count, cap), jnp.int32)],
        name="prep",
    )


def expert_kernel(parts, steps, apart, gate_ref, first_ref, second_ref, *refs):
    in_refs = refs[:parts]
    more_refs = dict(zip(apart, refs[parts:]))
    outs = refs[parts + len(apart) :]
    row_refs = outs[:parts]
    x_all, scaled, act_ref, pre_ref, gg_ref, y_all, total = outs[parts:]
    step = pl.program_id(0)
    slots = in_refs[0].shape[0] // 2

    @pl.when(step == 0)
    def _():
        for k in range(parts):
            place = slice(k * slots, (k + 1) * slots)
            value = in_refs[k][...]
            if k in more_refs:
                value = value + more_refs[k][...]
            x_all[place, :] = value[:slots, :]
            y_rows = value[slots:, :]
            y_all[place, :] = y_rows
            scaled[place, :] = (gate_ref[place, :] * y_rows.astype(F32)).astype(BF)
        gg_ref[...] = jnp.zeros_like(gg_ref)
        total[...] = jnp.zeros_like(total)

    first = first_ref[...]
    second = second_ref[...]
    u = dot(x_all[...], first)
    back = dot(y_all[...], second, LAST_LAST)
    square = u * u
    t = jnp.tanh(u * (ROOT + (ROOT * CUBE) * square))
    half = 0.5 + 0.5 * t
    act = (u * half).astype(BF)
    slope = half + u * (1.0 - t * t) * (0.5 * ROOT + (1.5 * ROOT * CUBE) * square)
    act_ref[...] = act
    gg_ref[...] += jnp.sum(act.astype(F32) * back, axis=1, keepdims=True)
    pre = (gate_ref[...] * back * slope).astype(BF)
    pre_ref[...] = pre
    total[...] += dot(pre, first, LAST_LAST)

    @pl.when(step == steps - 1)
    def _():
        for k in range(parts):
            row_refs[k][0] = total[k * slots : (k + 1) * slots, :].astype(BF)


def expert(blocks, gates, weight_in, weight_out, more=(), after=()):
    more = dict(more)
    parts = len(blocks)
    _, slots, width = blocks[0][0].shape
    slots //= 2
    rows = parts * slots
    hidden = weight_in.shape[1]
    tile = 768 if hidden % 768 == 0 else hidden
    steps = hidden // tile
    fixed = lambda dims: pl.BlockSpec(dims, lambda i: (0, 0))
    outs = call(
        functools.partial(expert_kernel, parts, steps, tuple(more)),
        [shape((1, slots, width))] * parts
        + [
            shape((rows, width)),
            shape((rows, width)),
            shape((rows, hidden)),
            shape((rows, hidden)),
            shape((rows, 1), F32),
        ],
        [
            fixed((rows, 1)),
            pl.BlockSpec((width, tile), lambda i: (0, i)),
            pl.BlockSpec((tile, width), lambda i: (i, 0)),
        ]
        + block_specs([*blocks, *more.values()], (2 * slots, width), lambda i: (0, 0)),
        [gates, weight_in, weight_out, *arrays(blocks), *arrays(more.values())],
        flops=6 * rows * width * hidden,
        nbytes=4 * width * hidden + 4 * rows * hidden + 8 * rows * width,
        after=after,
        grid=(steps,),
        out_specs=[pl.BlockSpec((1, slots, width), lambda i: (0, 0, 0))] * parts
        + [
            fixed((rows, width)),
            fixed((rows, width)),
            pl.BlockSpec((rows, tile), lambda i: (0, i)),
            pl.BlockSpec((rows, tile), lambda i: (0, i)),
            fixed((rows, 1)),
        ],
        scratch_shapes=[pltpu.VMEM((rows, width), BF), pltpu.VMEM((rows, width), F32)],
        name="expert",
    )
    return outs[:parts], outs[parts:]


def weight_kernel(turn, near_left, near_right, far_left, far_right, out_ref):
    left, right = (near_left, far_left), (near_right, far_right)
    value = sum(dot(a[...], b[...], FIRST_FIRST) for a, b in zip(left, right))
    out_ref[...] = value.astype(BF)


def weight_gradient(near, far, hidden_first, after=()):
    width, hidden = near[0].shape[1], near[1].shape[1]
    tile = 768 if hidden % 768 == 0 else hidden
    args, specs = [], []
    for rows, units in (near, far):
        all_rows = pl.BlockSpec(rows.shape, lambda i: (0, 0))
        some = pl.BlockSpec((units.shape[0], tile), lambda i: (0, i))
        args += [units, rows] if hidden_first else [rows, units]
        specs += [some, all_rows] if hidden_first else [all_rows, some]
    out, out_spec = (width, hidden), pl.BlockSpec((width, tile), lambda i: (0, i))
    if hidden_first:
        out, out_spec = (hidden, width), pl.BlockSpec((tile, width), lambda i: (i, 0))
    return call(
        functools.partial(weight_kernel, hidden_first),
        shape(out),
        specs,
        args,
        flops=4 * near[0].shape[0] * width * hidden,
        nbytes=2 * width * hidden,
        after=after,
        grid=(hidden // tile,),
        out_specs=out_spec,
        name="weight_gradient",
    )


def combine_kernel(count, parts, plus, me_ref, hit_ref, *refs):
    rows = jnp.concatenate([ref[...] for ref in refs[:parts]], axis=0)
    refs = refs[parts:]
    if plus:
        y_ref, refs = refs[0], refs[1:]
    outs, total = refs[: count // 2], refs[count // 2]
    total[...] = dot(hit_ref[...], rows, FIRST_FIRST)
    piece = outs[0].shape[1]
    for k in range(count):
        place = pl.ds(pl.multiple_of((me_ref[0] ^ k) * piece, piece), piece)
        value = total[place, :]
        if plus:
            value = value + y_ref[place, :].astype(F32)
        outs[k // 2][k % 2] = value.astype(BF)


def combine(me, hit, blocks, y, count, after=(), carry=None):
    parts = len(blocks)
    _, slots, width = blocks[0][0].shape
    tok = hit.shape[1]
    plus = [] if y is None else [y]
    rows = parts * slots
    return call(
        functools.partial(combine_kernel, count, parts, bool(plus)),
        [shape((2, tok // count, width))] * (count // 2),
        [SMEM, pl.BlockSpec((rows, tok), lambda i: (0, 0))]
        + block_specs(blocks, (slots, width), lambda i: (0, 0))
        + [pl.BlockSpec(b.shape, lambda i: (0, 0)) for b in plus],
        [me, hit, *arrays(blocks), *plus],
        flops=2 * rows * tok * width,
        nbytes=6 * tok * width,
        after=after,
        carry=carry,
        grid=(1,),
        out_specs=[pl.BlockSpec((2, tok // count, width), lambda i: (0, 0, 0))] * (count // 2),
        scratch_shapes=[pltpu.VMEM((tok, width), F32)],
        name="combine",
    )


def windows(width):
    size = width // HEADS
    for head in range(HEADS):
        start, stop = head * size, (head + 1) * size
        low, high = start // LANES, -(-stop // LANES)
        yield head, start, stop, low, high, slice(low * LANES, min(high * LANES, width))


def head_lanes(start, stop, window):
    lane = lax.broadcasted_iota(jnp.int32, (1, window.stop - window.start), 1) + window.start
    return (lane >= start) & (lane < stop)


def keep(held, part, inside, low, high):
    for tile in range(low, high):
        lanes = slice((tile - low) * LANES, min((tile - low + 1) * LANES, part.shape[1]))
        new = part[:, lanes]
        if held[tile] is not None:
            new = jnp.where(inside[:, lanes], new, held[tile])
        held[tile] = new


def probs_kernel(q_ref, k_ref, probs_ref, turned_ref):
    frames, patches, width = q_ref.shape
    rows = frames * patches
    scale = (width // HEADS) ** -0.5
    query = q_ref[...].reshape(rows, width)
    keys = k_ref[...].reshape(rows, width)
    same = (lax.broadcasted_iota(jnp.int32, (rows, rows), 0) % patches) == (
        lax.broadcasted_iota(jnp.int32, (rows, rows), 1) % patches
    )
    for head, start, stop, low, high, window in windows(width):
        inside = head_lanes(start, stop, window)
        q_win = jnp.where(inside, query[:, window], jnp.zeros((), BF))
        scores = jnp.where(same, dot(q_win, keys[:, window], LAST_LAST) * scale, -1e30)
        probs = jnp.exp(scores - jnp.max(scores, axis=1, keepdims=True))
        probs = probs / jnp.sum(probs, axis=1, keepdims=True)
        probs_ref[0, head] = probs
        turned_ref[0, head] = probs.T.astype(BF)


def patch_tile(frames, patches):
    return 16 if patches % 16 == 0 else patches


def probabilities(query, keys, after=()):
    frames, patches, width = query.shape
    tile = patch_tile(frames, patches)
    steps = patches // tile
    rows = frames * tile
    wide = pl.BlockSpec((frames, tile, width), lambda i: (0, i, 0))
    square = pl.BlockSpec((1, HEADS, rows, rows), lambda i: (i, 0, 0, 0))
    return call(
        probs_kernel,
        [shape((steps, HEADS, rows, rows), F32), shape((steps, HEADS, rows, rows))],
        [wide, wide],
        [query, keys],
        flops=8 * frames * patches * rows * width,
        nbytes=4 * frames * patches * width + 6 * steps * HEADS * rows * rows,
        after=after,
        grid=(steps,),
        out_specs=[square, square],
        name="probs",
    )


def meet_kernel(chips, *refs):
    near, far, out_ref = refs[:chips], refs[chips : 2 * chips], refs[2 * chips]
    for i in range(chips):
        value = near[i][...].astype(F32) + far[i ^ (chips // 2)][...].astype(F32)
        out_ref[i] = value.astype(BF)


def meet(near, far, carry):
    chips = len(near)
    _, piece, width = near[0].shape
    spec = pl.BlockSpec((None, piece, width), lambda i: (1, 0, 0))
    return call(
        functools.partial(meet_kernel, chips),
        [shape((chips, piece, width))],
        [spec] * (2 * chips),
        [*near, *far],
        nbytes=6 * chips * piece * width,
        carry=carry,
        grid=(1,),
        out_specs=[pl.BlockSpec((chips, piece, width), lambda i: (0, 0, 0))],
        name="meet",
    )


def value_kernel(count, me_ref, turned_ref, odd_ref, *refs):
    chips = count // 2
    near, far, refs = refs[:chips], refs[chips : 2 * chips], refs[2 * chips :]
    outs = refs[:count]
    grad_ref, result = refs[count:]
    me = me_ref[0]
    frames, patches, width = grad_ref.shape
    rows = frames * patches
    for i in range(chips):
        value = near[i][...].astype(F32) + far[i ^ (chips // 2)][...].astype(F32)
        grad_ref[me ^ (2 * i)] = value.astype(BF)
        grad_ref[me ^ (2 * i + 1)] = odd_ref[i]
    grad = grad_ref[...].reshape(rows, width)
    held = [None] * -(-width // LANES)
    for head, start, stop, low, high, window in windows(width):
        inside = head_lanes(start, stop, window)
        keep(held, dot(turned_ref[0, head], grad[:, window]), inside, low, high)
    for tile, value in enumerate(held):
        lanes = slice(tile * LANES, tile * LANES + value.shape[1])
        result[:, :, lanes] = value.astype(BF).reshape(frames, patches, value.shape[1])
    for k in range(count):
        outs[k][0] = result[me ^ k]


def value_gradient(me, turned, odd, near, far, count, after=()):
    _, piece, width = near[0].shape
    steps, _, rows, _ = turned.shape
    tile = piece // steps
    frames = rows // tile
    wide = pl.BlockSpec((frames, tile, width), lambda i: (0, i, 0))
    even = pl.BlockSpec((None, tile, width), lambda i: (0, i, 0))
    outs = call(
        functools.partial(value_kernel, count),
        [shape((1, piece, width))] * count + [shape((frames, piece, width))],
        [
            SMEM,
            pl.BlockSpec((1, HEADS, rows, rows), lambda i: (i, 0, 0, 0)),
            pl.BlockSpec((count // 2, tile, width), lambda i: (0, i, 0)),
        ]
        + [even] * (2 * len(near)),
        [me, turned, odd, *near, *far],
        flops=4 * frames * piece * rows * width,
        nbytes=8 * frames * piece * width,
        after=after,
        grid=(steps,),
        out_specs=[pl.BlockSpec((1, tile, width), lambda i: (0, i, 0))] * count + [wide],
        scratch_shapes=[pltpu.VMEM((frames, tile, width), BF)],
        name="value_gradient",
    )
    return outs[:count], outs[count]


def pair_kernel(count, me_ref, probs_ref, grad_ref, q_ref, k_ref, v_ref, *refs):
    outs, result = refs[:count], refs[count]
    me = me_ref[0]
    frames, patches, width = q_ref.shape
    rows = frames * patches
    scale = (width // HEADS) ** -0.5
    query, keys, values, grad = (
        ref[...].reshape(rows, width) for ref in (q_ref, k_ref, v_ref, grad_ref)
    )
    tiles = -(-width // LANES)
    held = [[None] * tiles for _ in range(2)]
    for head, start, stop, low, high, window in windows(width):
        inside = head_lanes(start, stop, window)
        g_win = jnp.where(inside, grad[:, window], jnp.zeros((), BF))
        prob_grad = dot(g_win, values[:, window], LAST_LAST)
        probs = probs_ref[0, head]
        delta = jnp.sum(probs * prob_grad, axis=1, keepdims=True)
        score_grad = (probs * (prob_grad - delta)).astype(BF)
        keep(held[0], dot(score_grad, keys[:, window]) * scale, inside, low, high)
        keep(held[1], dot(score_grad, query[:, window], FIRST_FIRST) * scale, inside, low, high)
    for which in range(2):
        for tile, value in enumerate(held[which]):
            lanes = slice(tile * LANES, tile * LANES + value.shape[1])
            value = value.astype(BF).reshape(frames, patches, value.shape[1])
            result[which, :, :, lanes] = value
    for k in range(count):
        for which in range(2):
            outs[k][0, which] = result[which, me ^ k]


def pair_gradients(me, probs, grad, query, keys, values, count, after=()):
    frames, piece, width = query.shape
    steps, _, rows, _ = probs.shape
    tile = piece // steps
    wide = pl.BlockSpec((frames, tile, width), lambda i: (0, i, 0))
    return call(
        functools.partial(pair_kernel, count),
        [shape((1, 2, piece, width))] * count,
        [SMEM, pl.BlockSpec((1, HEADS, rows, rows), lambda i: (i, 0, 0, 0))] + [wide] * 4,
        [me, probs, grad, query, keys, values],
        flops=12 * frames * piece * rows * width,
        nbytes=16 * frames * piece * width,
        after=after,
        grid=(steps,),
        out_specs=[pl.BlockSpec((1, 2, tile, width), lambda i: (0, 0, i, 0))] * count,
        scratch_shapes=[pltpu.VMEM((2, frames, tile, width), BF)],
        name="pair_gradients",
    )


def spread(count):
    half, quarter = count // 2, count // 4
    far = [k for i in range(quarter) for k in (half + quarter + i, half + i)]
    return far + list(range(half - 1, -1, -1))


def place_kernel(order, outs_count, me_ref, *refs):
    blocks, outs = refs[: len(order)], refs[len(order) :]
    piece = blocks[0].shape[-2]
    for k, block in zip(order, blocks):
        place = pl.ds(pl.multiple_of((me_ref[0] ^ k) * piece, piece), piece)
        if outs_count == 1:
            outs[0][place, :] = block[...]
        else:
            for which in range(outs_count):
                outs[which][place, :] = block[which]


def place(me, blocks, after=()):
    count = len(blocks)
    dims = blocks[0][0].shape[1:]
    tok = count * dims[-2]
    outs_count = dims[0] if len(dims) == 3 else 1
    order = spread(count)
    blocks = [blocks[k] for k in order]
    return call(
        functools.partial(place_kernel, order, outs_count),
        [shape((tok, dims[-1]))] * outs_count,
        [SMEM] + block_specs(blocks, dims, lambda i: (0,) * len(dims)),
        [me, *arrays(blocks)],
        nbytes=4 * outs_count * tok * dims[-1],
        after=after,
        grid=(1,),
        out_specs=[pl.BlockSpec((tok, dims[-1]), lambda i: (0, 0))] * outs_count,
        name="place",
    )


def body(
    layer_input,
    output_grad,
    expert_lists,
    gate_values,
    weight_in,
    weight_out,
    query_rows,
    key_rows,
    value_rows,
):
    count = lax.axis_size("dev")
    index = lax.axis_index("dev").astype(jnp.int32)
    me = index.reshape(1)
    frames_here, patches, width = layer_input.shape
    tok = frames_here * patches
    cap = expert_lists.shape[2]
    group = count // 2
    x = layer_input.reshape(tok, width)
    y = output_grad.reshape(tok, width)
    first, second = weight_in[0], weight_out[0]
    pairs = functools.partial(exchange_pairs, me=index, count=count)

    *send, hit_mine, hit_other, gates, key = prep(
        me, expert_lists[0], gate_values[0], x, y, group
    )
    slots = send[0].shape[1] // 2
    half = group * slots
    single = functools.partial(exchange_single, me=index, count=count)
    got_near = single(send[:group], 0)
    got_far = single(send[group:], group)
    more, early = {}, got_far[::2]
    if count == 8:
        split = group // 2
        away, close = exchange_apart(send[group + split], group + split, count)
        got_far[split], more[split] = (away, 0), (close, 0)
        early = [got_far[0], got_far[split]]

    probs, turned = probabilities(query_rows, key_rows, after=[hit_mine])
    rows_near, rest_near = expert(
        got_near, gates[:half], first, second, after=[turned, *arrays(early)]
    )
    back_near = single(rows_near, 0)
    late = arrays(got_far[1::2]) + arrays(more.values())
    send_near = combine(me, hit_mine, back_near, y, count, after=late)
    grad_near = pairs(send_near)
    rows_far, rest_far = expert(
        got_far, gates[half:], first, second, more=more, after=send_near[:1]
    )
    back_far = single(rows_far, 0)

    x_near, scaled_near, act_near, pre_near, sums_near = rest_near
    x_far, scaled_far, act_far, pre_far, sums_far = rest_far
    crossed = grad_near[2:]
    in_term = weight_gradient((x_near, pre_near), (x_far, pre_far), False)
    *send_far, in_term = combine(
        me, hit_other, back_far, None, count, after=crossed, carry=in_term
    )
    in_share = lax.psum_scatter(in_term, "slab", scatter_dimension=0, tiled=True).astype(F32)
    grad_far = pairs(send_far)
    out_term = weight_gradient(
        (scaled_near, act_near), (scaled_far, act_far), True, after=send_far[:1]
    )
    slot_sums = jnp.concatenate([sums_near, sums_far]).reshape(count, slots, 1)
    slot_ids = jnp.arange(slots, dtype=jnp.int32)[None, :, None]
    gate_grad = jnp.sum(jnp.where(key[:, None, :] == slot_ids, slot_sums, 0.0), axis=(0, 1))

    odd, out_term = meet(grad_near, grad_far, out_term)
    out_share = lax.psum_scatter(out_term, "slab", scatter_dimension=0, tiled=True).astype(F32)
    odd = other_core(odd, count)
    value_send, grad_attn = value_gradient(me, turned, odd, grad_near, grad_far, count)
    pair_send = pair_gradients(me, probs, grad_attn, query_rows, key_rows, value_rows, count)
    (value_grad,) = place(me, single(value_send, 0), after=pair_send[:1])
    query_grad, key_grad = place(me, single(pair_send, 0), after=[in_share])
    whole = (frames_here, patches, width)
    return (
        gate_grad.reshape(1, 1, cap),
        in_share[None],
        out_share[None],
        query_grad.reshape(whole),
        key_grad.reshape(whole),
        value_grad.reshape(whole),
    )


def solution(mesh):
    return jax.shard_map(
        body,
        mesh=mesh,
        in_specs=(
            P("dev", "slab", None),
            P("dev", "slab", None),
            P("slab", None, None),
            P("slab", "dev", None),
            P("dev", None, None),
            P("dev", None, None),
            P(None, ("slab", "dev"), None),
            P(None, ("slab", "dev"), None),
            P(None, ("slab", "dev"), None),
        ),
        out_specs=(
            P("slab", "dev", None),
            P("dev", "slab", None),
            P("dev", "slab", None),
            P("dev", "slab", None),
            P("dev", "slab", None),
            P("dev", "slab", None),
        ),
        check_vma=False,
    )
```

```python
import functools

import jax
import jax.numpy as jnp
from jax import lax
from jax.experimental import pallas as pl
from jax.experimental.pallas import tpu as pltpu
from jax.sharding import PartitionSpec as P

HEADS = 16
LANES = 128
ROOT = 0.7978845608028654
CUBE = 0.044715
BF = jnp.bfloat16
F32 = jnp.float32
VMEM_LIMIT = 56 * 1024 * 1024

ROWS_COLS = (((1,), (0,)), ((), ()))
LAST_LAST = (((1,), (1,)), ((), ()))
FIRST_FIRST = (((0,), (0,)), ((), ()))


def dot(left, right, dims=ROWS_COLS):
    return lax.dot_general(left, right, dims, preferred_element_type=F32)


def call(kernel, out_shape, in_specs, args, out_specs, after=(), carry=None, flops=0, nbytes=0, **kwargs):
    held = list(after) if carry is None else [*after, carry]
    skip = len(args)
    aliases = {}
    if carry is not None:
        aliases = {skip + len(held) - 1: len(out_shape)}
        out_shape = [*out_shape, jax.ShapeDtypeStruct(carry.shape, carry.dtype)]
        out_specs = [*out_specs, ANY]

    def run(*refs):
        refs = [*refs[:skip], *refs[skip + len(held) :]]
        if carry is not None:
            del refs[skip + len(out_shape) - 1]
        kernel(*refs)

    return pl.pallas_call(
        run,
        out_shape=out_shape,
        in_specs=list(in_specs) + [ANY] * len(held),
        out_specs=out_specs,
        input_output_aliases=aliases,
        compiler_params=pltpu.CompilerParams(vmem_limit_bytes=VMEM_LIMIT),
        cost_estimate=pl.CostEstimate(flops=flops, bytes_accessed=nbytes, transcendentals=0),
        **kwargs,
    )(*args, *held)


ANY = pl.BlockSpec(memory_space=pl.ANY)
SMEM = pl.BlockSpec(memory_space=pltpu.SMEM)
WHOLE = pl.BlockSpec(memory_space=pltpu.VMEM)


def shape(dims, dtype=BF):
    return jax.ShapeDtypeStruct(dims, dtype)


def exchange_all(blocks, which, me, count):
    size = len(which)
    first = which[0]
    order = me ^ first
    groups = None
    if size < count:
        groups = [[g * size + j for j in range(size)] for g in range(count // size)]
    places = (order % size) ^ jnp.arange(size, dtype=jnp.int32)
    stacked = jnp.stack(blocks)[places]
    if first:
        across = [(i, i ^ first) for i in range(count)]
        stacked = lax.ppermute(stacked, "dev", across)
        places = (me % size) ^ jnp.arange(size, dtype=jnp.int32)
    got = lax.all_to_all(stacked, "dev", 0, 0, axis_index_groups=groups, tiled=True)[places]
    return [got[i] for i in range(size)]


def exchange_pairs(pairs, me, count):
    if count > 8:
        blocks = exchange_all([pair[j] for pair in pairs for j in range(2)], list(range(count)), me, count)
        mates = other_core(jnp.stack(blocks[1::2]), count)
        return [jnp.stack([block, mates[i]]) for i, block in enumerate(blocks[::2])]
    return [
        lax.ppermute(pair, "dev", [(d, d ^ (2 * i)) for d in range(count)]) if i else pair
        for i, pair in enumerate(pairs)
    ]


def other_core(array, count):
    return lax.ppermute(array, "dev", [(d, d ^ 1) for d in range(count)])


def exchange_single(blocks, first, me, count):
    which = list(range(first, first + len(blocks)))
    if count > 8:
        got = exchange_all([b[0] for b in blocks], which, me, count)
        return [(block[None], 0) for block in got]
    pairs = {k: [(d, d ^ k) for d in range(count)] for k in which}
    return [(lax.ppermute(b, "dev", pairs[k]) if k else b, 0) for b, k in zip(blocks, which)]


def exchange_apart(block, k, count):
    pairs = [(d, d ^ k) for d in range(count)]
    far = [(d, e) for d, e in pairs if abs(d - e) > count // 2]
    near = [(d, e) for d, e in pairs if abs(d - e) <= count // 2]
    return lax.ppermute(block, "dev", far), lax.ppermute(block, "dev", near)


def arrays(got):
    return [array for array, _ in got]


def block_specs(got, block, index_map):
    return [
        pl.BlockSpec((None, *block), lambda *i, at=at: (at, *index_map(*i))) for _, at in got
    ]


def prep_kernel(count, group, slots, tok, me_ref, table_ref, gate_ref, x_ref, y_ref, *refs):
    send_refs = refs[:count]
    mine_ref, other_ref, gate_out, key_out, rank_ref = refs[count:]
    me = me_ref[0]
    cap = table_ref.shape[1]
    width = table_ref.shape[0]
    upper = lax.broadcasted_iota(jnp.int32, (cap, cap), 0) < lax.broadcasted_iota(
        jnp.int32, (cap, cap), 1
    )
    upper = upper.astype(F32).astype(BF)
    table = table_ref[...]
    slot_ids = lax.broadcasted_iota(jnp.int32, (slots, cap), 0)
    tok_ids = lax.broadcasted_iota(jnp.int32, (slots, tok), 1)

    def ranked(inside):
        rank = dot(inside.astype(F32).astype(BF), upper).astype(jnp.int32)
        return jnp.where(inside, rank, -1)

    def hits(frame, ks, out_ref):
        low = frame * tok
        rank_ref[...] = ranked((table >= low) & (table < low + tok))
        for place, k in enumerate(ks):
            row = rank_ref[pl.ds(me ^ k, 1), :]
            offset = table_ref[pl.ds(me ^ k, 1), :] - low
            found = jnp.where(row == slot_ids, (offset + 1).astype(F32), 0.0)
            column = (jnp.sum(found, axis=1, keepdims=True) - 1.0).astype(jnp.int32)
            out_ref[place * slots : (place + 1) * slots, :] = (
                (column == tok_ids).astype(F32).astype(BF)
            )

    hits(me, range(count), mine_ref)
    for half, source in enumerate((x_ref, y_ref)):
        rows = dot(mine_ref[...], source[...]).astype(BF)
        for k in range(count):
            send_refs[k][0, half * slots : (half + 1) * slots, :] = rows[
                k * slots : (k + 1) * slots
            ]
    hits(me ^ group, range(group), other_ref)

    mine_row = table_ref[pl.ds(me, 1), :]
    frames = (lax.broadcasted_iota(jnp.int32, (width, cap), 0) ^ me) * tok
    key = ranked((mine_row >= frames) & (mine_row < frames + tok))
    key_out[...] = key
    for k in range(count):
        found = jnp.where(key[k : k + 1, :] == slot_ids, gate_ref[...], 0.0)
        gate_out[k * slots : (k + 1) * slots, :] = jnp.sum(found, axis=1, keepdims=True)


def prep(me, table, gate_row, x, y, group):
    count, cap = table.shape
    tok, width = x.shape
    slots = 2 * cap // count
    return call(
        functools.partial(prep_kernel, count, group, slots, tok),
        [shape((1, 2 * slots, width))] * count
        + [
            shape((count * slots, tok)),
            shape((group * slots, tok)),
            shape((count * slots, 1), F32),
            shape((count, cap), jnp.int32),
        ],
        [SMEM, WHOLE, WHOLE, WHOLE, WHOLE],
        [me, table, gate_row, x, y],
        flops=4 * count * slots * tok * width,
        nbytes=8 * count * slots * width,
        out_specs=[WHOLE] * (count + 4),
        scratch_shapes=[pltpu.VMEM((count, cap), jnp.int32)],
        name="prep",
    )


def expert_kernel(parts, steps, apart, gate_ref, first_ref, second_ref, *refs):
    in_refs = refs[:parts]
    more_refs = dict(zip(apart, refs[parts:]))
    outs = refs[parts + len(apart) :]
    row_refs = outs[:parts]
    x_all, scaled, act_ref, pre_ref, gg_ref, y_all, total = outs[parts:]
    step = pl.program_id(0)
    slots = in_refs[0].shape[0] // 2

    @pl.when(step == 0)
    def _():
        for k in range(parts):
            place = slice(k * slots, (k + 1) * slots)
            value = in_refs[k][...]
            if k in more_refs:
                value = value + more_refs[k][...]
            x_all[place, :] = value[:slots, :]
            y_rows = value[slots:, :]
            y_all[place, :] = y_rows
            scaled[place, :] = (gate_ref[place, :] * y_rows.astype(F32)).astype(BF)
        gg_ref[...] = jnp.zeros_like(gg_ref)
        total[...] = jnp.zeros_like(total)

    first = first_ref[...]
    second = second_ref[...]
    u = dot(x_all[...], first)
    back = dot(y_all[...], second, LAST_LAST)
    square = u * u
    t = jnp.tanh(u * (ROOT + (ROOT * CUBE) * square))
    half = 0.5 + 0.5 * t
    act = (u * half).astype(BF)
    slope = half + u * (1.0 - t * t) * (0.5 * ROOT + (1.5 * ROOT * CUBE) * square)
    act_ref[...] = act
    gg_ref[...] += jnp.sum(act.astype(F32) * back, axis=1, keepdims=True)
    pre = (gate_ref[...] * back * slope).astype(BF)
    pre_ref[...] = pre
    total[...] += dot(pre, first, LAST_LAST)

    @pl.when(step == steps - 1)
    def _():
        for k in range(parts):
            row_refs[k][0] = total[k * slots : (k + 1) * slots, :].astype(BF)


def expert(blocks, gates, weight_in, weight_out, more=(), after=()):
    more = dict(more)
    parts = len(blocks)
    _, slots, width = blocks[0][0].shape
    slots //= 2
    rows = parts * slots
    hidden = weight_in.shape[1]
    tile = 768 if hidden % 768 == 0 else hidden
    steps = hidden // tile
    fixed = lambda dims: pl.BlockSpec(dims, lambda i: (0, 0))
    outs = call(
        functools.partial(expert_kernel, parts, steps, tuple(more)),
        [shape((1, slots, width))] * parts
        + [
            shape((rows, width)),
            shape((rows, width)),
            shape((rows, hidden)),
            shape((rows, hidden)),
            shape((rows, 1), F32),
        ],
        [
            fixed((rows, 1)),
            pl.BlockSpec((width, tile), lambda i: (0, i)),
            pl.BlockSpec((tile, width), lambda i: (i, 0)),
        ]
        + block_specs([*blocks, *more.values()], (2 * slots, width), lambda i: (0, 0)),
        [gates, weight_in, weight_out, *arrays(blocks), *arrays(more.values())],
        flops=6 * rows * width * hidden,
        nbytes=4 * width * hidden + 4 * rows * hidden + 8 * rows * width,
        after=after,
        grid=(steps,),
        out_specs=[pl.BlockSpec((1, slots, width), lambda i: (0, 0, 0))] * parts
        + [
            fixed((rows, width)),
            fixed((rows, width)),
            pl.BlockSpec((rows, tile), lambda i: (0, i)),
            pl.BlockSpec((rows, tile), lambda i: (0, i)),
            fixed((rows, 1)),
        ],
        scratch_shapes=[pltpu.VMEM((rows, width), BF), pltpu.VMEM((rows, width), F32)],
        name="expert",
    )
    return outs[:parts], outs[parts:]


def weight_kernel(turn, near_left, near_right, far_left, far_right, out_ref):
    left, right = (near_left, far_left), (near_right, far_right)
    value = sum(dot(a[...], b[...], FIRST_FIRST) for a, b in zip(left, right))
    out_ref[...] = value.astype(BF)


def weight_gradient(near, far, hidden_first, after=()):
    width, hidden = near[0].shape[1], near[1].shape[1]
    tile = 768 if hidden % 768 == 0 else hidden
    args, specs = [], []
    for rows, units in (near, far):
        all_rows = pl.BlockSpec(rows.shape, lambda i: (0, 0))
        some = pl.BlockSpec((units.shape[0], tile), lambda i: (0, i))
        args += [units, rows] if hidden_first else [rows, units]
        specs += [some, all_rows] if hidden_first else [all_rows, some]
    out, out_spec = (width, hidden), pl.BlockSpec((width, tile), lambda i: (0, i))
    if hidden_first:
        out, out_spec = (hidden, width), pl.BlockSpec((tile, width), lambda i: (i, 0))
    return call(
        functools.partial(weight_kernel, hidden_first),
        shape(out),
        specs,
        args,
        flops=4 * near[0].shape[0] * width * hidden,
        nbytes=2 * width * hidden,
        after=after,
        grid=(hidden // tile,),
        out_specs=out_spec,
        name="weight_gradient",
    )


def release_kernel(token_ref):
    token_ref[...] = jnp.zeros_like(token_ref)


def release(term, after):
    return call(
        release_kernel,
        [shape((8, LANES), F32)],
        [],
        [],
        out_specs=[WHOLE],
        after=after,
        carry=term,
        name="release",
    )


def widen_kernel(term_ref, out_ref):
    out_ref[...] = term_ref[...].astype(F32)


def widen(term):
    rows, width = term.shape
    tile = rows // 4 if rows % 64 == 0 else rows
    block = pl.BlockSpec((tile, width), lambda i: (i, 0))
    return call(
        widen_kernel,
        shape(term.shape, F32),
        [block],
        [term],
        nbytes=6 * rows * width,
        grid=(rows // tile,),
        out_specs=block,
        name="widen",
    )


def combine_kernel(count, parts, plus, me_ref, hit_ref, *refs):
    rows = jnp.concatenate([ref[...] for ref in refs[:parts]], axis=0)
    refs = refs[parts:]
    if plus:
        y_ref, refs = refs[0], refs[1:]
    outs, total = refs[: count // 2], refs[count // 2]
    total[...] = dot(hit_ref[...], rows, FIRST_FIRST)
    piece = outs[0].shape[1]
    for k in range(count):
        place = pl.ds(pl.multiple_of((me_ref[0] ^ k) * piece, piece), piece)
        value = total[place, :]
        if plus:
            value = value + y_ref[place, :].astype(F32)
        outs[k // 2][k % 2] = value.astype(BF)


def combine(me, hit, blocks, y, count, after=(), carry=None):
    parts = len(blocks)
    _, slots, width = blocks[0][0].shape
    tok = hit.shape[1]
    plus = [] if y is None else [y]
    rows = parts * slots
    return call(
        functools.partial(combine_kernel, count, parts, bool(plus)),
        [shape((2, tok // count, width))] * (count // 2),
        [SMEM, pl.BlockSpec((rows, tok), lambda i: (0, 0))]
        + block_specs(blocks, (slots, width), lambda i: (0, 0))
        + [pl.BlockSpec(b.shape, lambda i: (0, 0)) for b in plus],
        [me, hit, *arrays(blocks), *plus],
        flops=2 * rows * tok * width,
        nbytes=6 * tok * width,
        after=after,
        carry=carry,
        grid=(1,),
        out_specs=[pl.BlockSpec((2, tok // count, width), lambda i: (0, 0, 0))] * (count // 2),
        scratch_shapes=[pltpu.VMEM((tok, width), F32)],
        name="combine",
    )


def windows(width):
    size = width // HEADS
    for head in range(HEADS):
        start, stop = head * size, (head + 1) * size
        low, high = start // LANES, -(-stop // LANES)
        yield head, start, stop, low, high, slice(low * LANES, min(high * LANES, width))


def head_lanes(start, stop, window):
    lane = lax.broadcasted_iota(jnp.int32, (1, window.stop - window.start), 1) + window.start
    return (lane >= start) & (lane < stop)


def keep(held, part, inside, low, high):
    for tile in range(low, high):
        lanes = slice((tile - low) * LANES, min((tile - low + 1) * LANES, part.shape[1]))
        new = part[:, lanes]
        if held[tile] is not None:
            new = jnp.where(inside[:, lanes], new, held[tile])
        held[tile] = new


def probs_kernel(q_ref, k_ref, probs_ref, turned_ref):
    frames, patches, width = q_ref.shape
    rows = frames * patches
    scale = (width // HEADS) ** -0.5
    query = q_ref[...].reshape(rows, width)
    keys = k_ref[...].reshape(rows, width)
    same = (lax.broadcasted_iota(jnp.int32, (rows, rows), 0) % patches) == (
        lax.broadcasted_iota(jnp.int32, (rows, rows), 1) % patches
    )
    for head, start, stop, low, high, window in windows(width):
        inside = head_lanes(start, stop, window)
        q_win = jnp.where(inside, query[:, window], jnp.zeros((), BF))
        scores = jnp.where(same, dot(q_win, keys[:, window], LAST_LAST) * scale, -1e30)
        probs = jnp.exp(scores - jnp.max(scores, axis=1, keepdims=True))
        probs = probs / jnp.sum(probs, axis=1, keepdims=True)
        probs_ref[0, head] = probs
        turned_ref[0, head] = probs.T.astype(BF)


def patch_tile(frames, patches):
    return 16 if patches % 16 == 0 else patches


def probabilities(query, keys, after=()):
    frames, patches, width = query.shape
    tile = patch_tile(frames, patches)
    steps = patches // tile
    rows = frames * tile
    wide = pl.BlockSpec((frames, tile, width), lambda i: (0, i, 0))
    square = pl.BlockSpec((1, HEADS, rows, rows), lambda i: (i, 0, 0, 0))
    return call(
        probs_kernel,
        [shape((steps, HEADS, rows, rows), F32), shape((steps, HEADS, rows, rows))],
        [wide, wide],
        [query, keys],
        flops=8 * frames * patches * rows * width,
        nbytes=4 * frames * patches * width + 6 * steps * HEADS * rows * rows,
        after=after,
        grid=(steps,),
        out_specs=[square, square],
        name="probs",
    )


def meet_kernel(chips, *refs):
    far, near, out_ref = refs[:chips][::-1], refs[chips : 2 * chips][::-1], refs[2 * chips]
    for i in range(chips):
        value = near[i][...].astype(F32) + far[i ^ (chips // 2)][...].astype(F32)
        out_ref[i] = value.astype(BF)


def meet(near, far, carry):
    chips = len(near)
    _, piece, width = near[0].shape
    spec = pl.BlockSpec((None, piece, width), lambda i: (1, 0, 0))
    return call(
        functools.partial(meet_kernel, chips),
        [shape((chips, piece, width))],
        [spec] * (2 * chips),
        [*far[::-1], *near[::-1]],
        nbytes=6 * chips * piece * width,
        carry=carry,
        grid=(1,),
        out_specs=[pl.BlockSpec((chips, piece, width), lambda i: (0, 0, 0))],
        name="meet",
    )


def value_kernel(count, me_ref, turned_ref, odd_ref, *refs):
    chips = count // 2
    near, far, refs = refs[:chips], refs[chips : 2 * chips], refs[2 * chips :]
    outs = refs[:count]
    grad_ref, result = refs[count:]
    me = me_ref[0]
    frames, patches, width = grad_ref.shape
    rows = frames * patches
    for i in range(chips):
        value = near[i][...].astype(F32) + far[i ^ (chips // 2)][...].astype(F32)
        grad_ref[me ^ (2 * i)] = value.astype(BF)
        grad_ref[me ^ (2 * i + 1)] = odd_ref[i]
    grad = grad_ref[...].reshape(rows, width)
    held = [None] * -(-width // LANES)
    for head, start, stop, low, high, window in windows(width):
        inside = head_lanes(start, stop, window)
        keep(held, dot(turned_ref[0, head], grad[:, window]), inside, low, high)
    for tile, value in enumerate(held):
        lanes = slice(tile * LANES, tile * LANES + value.shape[1])
        result[:, :, lanes] = value.astype(BF).reshape(frames, patches, value.shape[1])
    for k in range(count):
        outs[k][0] = result[me ^ k]


def value_gradient(me, turned, odd, near, far, count, after=()):
    _, piece, width = near[0].shape
    steps, _, rows, _ = turned.shape
    tile = piece // steps
    frames = rows // tile
    wide = pl.BlockSpec((frames, tile, width), lambda i: (0, i, 0))
    even = pl.BlockSpec((None, tile, width), lambda i: (0, i, 0))
    outs = call(
        functools.partial(value_kernel, count),
        [shape((1, piece, width))] * count + [shape((frames, piece, width))],
        [
            SMEM,
            pl.BlockSpec((1, HEADS, rows, rows), lambda i: (i, 0, 0, 0)),
            pl.BlockSpec((count // 2, tile, width), lambda i: (0, i, 0)),
        ]
        + [even] * (2 * len(near)),
        [me, turned, odd, *near, *far],
        flops=4 * frames * piece * rows * width,
        nbytes=8 * frames * piece * width,
        after=after,
        grid=(steps,),
        out_specs=[pl.BlockSpec((1, tile, width), lambda i: (0, i, 0))] * count + [wide],
        scratch_shapes=[pltpu.VMEM((frames, tile, width), BF)],
        name="value_gradient",
    )
    return outs[:count], outs[count]


def pair_kernel(count, me_ref, probs_ref, grad_ref, q_ref, k_ref, v_ref, *refs):
    outs, result = refs[:count], refs[count]
    me = me_ref[0]
    frames, patches, width = q_ref.shape
    rows = frames * patches
    scale = (width // HEADS) ** -0.5
    query, keys, values, grad = (
        ref[...].reshape(rows, width) for ref in (q_ref, k_ref, v_ref, grad_ref)
    )
    tiles = -(-width // LANES)
    held = [[None] * tiles for _ in range(2)]
    for head, start, stop, low, high, window in windows(width):
        inside = head_lanes(start, stop, window)
        g_win = jnp.where(inside, grad[:, window], jnp.zeros((), BF))
        prob_grad = dot(g_win, values[:, window], LAST_LAST)
        probs = probs_ref[0, head]
        delta = jnp.sum(probs * prob_grad, axis=1, keepdims=True)
        score_grad = (probs * (prob_grad - delta)).astype(BF)
        keep(held[0], dot(score_grad, keys[:, window]) * scale, inside, low, high)
        keep(held[1], dot(score_grad, query[:, window], FIRST_FIRST) * scale, inside, low, high)
    for which in range(2):
        for tile, value in enumerate(held[which]):
            lanes = slice(tile * LANES, tile * LANES + value.shape[1])
            value = value.astype(BF).reshape(frames, patches, value.shape[1])
            result[which, :, :, lanes] = value
    for k in range(count):
        for which in range(2):
            outs[k][0, which] = result[which, me ^ k]


def pair_gradients(me, probs, grad, query, keys, values, count, after=()):
    frames, piece, width = query.shape
    steps, _, rows, _ = probs.shape
    tile = piece // steps
    wide = pl.BlockSpec((frames, tile, width), lambda i: (0, i, 0))
    return call(
        functools.partial(pair_kernel, count),
        [shape((1, 2, piece, width))] * count,
        [SMEM, pl.BlockSpec((1, HEADS, rows, rows), lambda i: (i, 0, 0, 0))] + [wide] * 4,
        [me, probs, grad, query, keys, values],
        flops=12 * frames * piece * rows * width,
        nbytes=16 * frames * piece * width,
        after=after,
        grid=(steps,),
        out_specs=[pl.BlockSpec((1, 2, tile, width), lambda i: (0, 0, i, 0))] * count,
        scratch_shapes=[pltpu.VMEM((2, frames, tile, width), BF)],
        name="pair_gradients",
    )


def spread(count):
    half, quarter = count // 2, count // 4
    far = [k for i in range(quarter) for k in (half + quarter + i, half + i)]
    return far + list(range(half - 1, -1, -1))


def place_kernel(order, outs_count, me_ref, *refs):
    blocks, outs = refs[: len(order)], refs[len(order) :]
    piece = blocks[0].shape[-2]
    for k, block in zip(order, blocks):
        place = pl.ds(pl.multiple_of((me_ref[0] ^ k) * piece, piece), piece)
        if outs_count == 1:
            outs[0][place, :] = block[...]
        else:
            for which in range(outs_count):
                outs[which][place, :] = block[which]


def place(me, blocks, after=()):
    count = len(blocks)
    dims = blocks[0][0].shape[1:]
    tok = count * dims[-2]
    outs_count = dims[0] if len(dims) == 3 else 1
    order = spread(count)
    blocks = [blocks[k] for k in order]
    return call(
        functools.partial(place_kernel, order, outs_count),
        [shape((tok, dims[-1]))] * outs_count,
        [SMEM] + block_specs(blocks, dims, lambda i: (0,) * len(dims)),
        [me, *arrays(blocks)],
        nbytes=4 * outs_count * tok * dims[-1],
        after=after,
        grid=(1,),
        out_specs=[pl.BlockSpec((tok, dims[-1]), lambda i: (0, 0))] * outs_count,
        name="place",
    )


def body(
    layer_input,
    output_grad,
    expert_lists,
    gate_values,
    weight_in,
    weight_out,
    query_rows,
    key_rows,
    value_rows,
):
    count = lax.axis_size("dev")
    index = lax.axis_index("dev").astype(jnp.int32)
    me = index.reshape(1)
    frames_here, patches, width = layer_input.shape
    tok = frames_here * patches
    cap = expert_lists.shape[2]
    group = count // 2
    x = layer_input.reshape(tok, width)
    y = output_grad.reshape(tok, width)
    first, second = weight_in[0], weight_out[0]
    pairs = functools.partial(exchange_pairs, me=index, count=count)

    *send, hit_mine, hit_other, gates, key = prep(
        me, expert_lists[0], gate_values[0], x, y, group
    )
    slots = send[0].shape[1] // 2
    half = group * slots
    single = functools.partial(exchange_single, me=index, count=count)
    got_near = single(send[:group], 0)
    got_far = single(send[group:], group)
    more, early = {}, got_far[::2]
    if count == 8:
        split = group // 2
        away, close = exchange_apart(send[group + split], group + split, count)
        got_far[split], more[split] = (away, 0), (close, 0)
        early = [got_far[0], got_far[split]]

    probs, turned = probabilities(query_rows, key_rows, after=[hit_mine])
    rows_near, rest_near = expert(
        got_near, gates[:half], first, second, after=[turned, *arrays(early)]
    )
    back_near = single(rows_near, 0)
    late = arrays(got_far[1::2]) + arrays(more.values())
    send_near = combine(me, hit_mine, back_near, y, count, after=late)
    grad_near = pairs(send_near)
    rows_far, rest_far = expert(
        got_far, gates[half:], first, second, more=more, after=send_near[:1]
    )
    back_far = single(rows_far, 0)

    x_near, scaled_near, act_near, pre_near, sums_near = rest_near
    x_far, scaled_far, act_far, pre_far, sums_far = rest_far
    crossed = grad_near[2:]
    in_term = weight_gradient((x_near, pre_near), (x_far, pre_far), False)
    token, in_term = release(in_term, [*arrays(back_far), *crossed])
    in_share = lax.psum_scatter(in_term, "slab", scatter_dimension=0, tiled=True).astype(F32)
    send_far = combine(me, hit_other, back_far, None, count, after=[token])
    grad_far = pairs(send_far)
    out_term = weight_gradient(
        (scaled_near, act_near), (scaled_far, act_far), True, after=send_far[:1]
    )
    slot_sums = jnp.concatenate([sums_near, sums_far]).reshape(count, slots, 1)
    slot_ids = jnp.arange(slots, dtype=jnp.int32)[None, :, None]
    gate_grad = jnp.sum(jnp.where(key[:, None, :] == slot_ids, slot_sums, 0.0), axis=(0, 1))

    odd, out_term = meet(grad_near, grad_far, out_term)
    out_share = widen(lax.psum_scatter(out_term, "slab", scatter_dimension=0, tiled=True))
    odd = other_core(odd, count)
    value_send, grad_attn = value_gradient(me, turned, odd, grad_near, grad_far, count)
    pair_send = pair_gradients(me, probs, grad_attn, query_rows, key_rows, value_rows, count)
    (value_grad,) = place(me, single(value_send, 0), after=pair_send[:1])
    query_grad, key_grad = place(me, single(pair_send, 0), after=[in_share])
    whole = (frames_here, patches, width)
    return (
        gate_grad.reshape(1, 1, cap),
        in_share[None],
        out_share[None],
        query_grad.reshape(whole),
        key_grad.reshape(whole),
        value_grad.reshape(whole),
    )


def solution(mesh):
    return jax.shard_map(
        body,
        mesh=mesh,
        in_specs=(
            P("dev", "slab", None),
            P("dev", "slab", None),
            P("slab", None, None),
            P("slab", "dev", None),
            P("dev", None, None),
            P("dev", None, None),
            P(None, ("slab", "dev"), None),
            P(None, ("slab", "dev"), None),
            P(None, ("slab", "dev"), None),
        ),
        out_specs=(
            P("slab", "dev", None),
            P("dev", "slab", None),
            P("dev", "slab", None),
            P("dev", "slab", None),
            P("dev", "slab", None),
            P("dev", "slab", None),
        ),
        check_vma=False,
    )
```
